256 devices in a mesh: front: 4 (over x), row: 4 (over y), col: 16 (over z, core).
Axes of the slice: x: 4, y: 4, z: 8, core: 2. Of those that a mesh axis runs over, the one named last changes fastest.
Arguments:
- child_rhs: float32 [4, 8192, 128], P('front', 'col'), may hold values from -6 to 6
- root_rhs: float32 [12288, 128], P('col'), may hold values from -6 to 6
- child_inv: float32 [4, 8192, 8192], P('front', 'row', 'col'), may hold values from -0.0625 to 0.0625
- coupling: float32 [4, 8192, 6144], P('front', 'row', 'col'), may hold values from -0.0625 to 0.0625
- root_inv: float32 [12288, 12288], P(('front', 'row'), 'col'), may hold values from -0.0546875 to 0.0546875
- pivot_counts: int32 [4], replicated, may hold values from 4096 to 8192, as said below
- border_map: int32 [4, 6144], P('front', 'col'), may hold values from 0 to 12287, as said below
Outputs:
- child_solution: float32 [4, 8192, 128], P('front', 'col')
- root_solution: float32 [12288, 128], P('col')
The draws below stay inside these ranges and needn't reach their ends.
Inputs may be any that keep to these rules, and one draw needn't show every extreme that they name: `pivot_counts`: each child front has 4096 to 8192 live pivots; some front has exactly 8192 in every draw. `border_map`: border rows of one front map to distinct root rows; the k-th of 16 equal blocks of border rows maps into the k-th of 16 equal blocks of root rows.
All inputs are finite; a program needn't handle non-finite values.
Results may differ from the reference program's by a relative error of at most 0.0001.
Values sent between devices are 32-bit elements; how exact they have to be, the bound alone decides.
A program may use at most 64 MiB of HBM per device.

```python
import jax
import jax.numpy as jnp
from jax import lax

PMAX = 8192
BORDER = 6144
ROOT = 12288
NRHS = 128
FRONTS = 4
N_COL = 16


def draw_pivot_counts(key, part):
    key = jax.random.fold_in(key, 11)
    first, second = jax.random.split(key)
    counts = jax.random.randint(first, (FRONTS,), PMAX // 2, PMAX + 1)
    fullest = jax.random.randint(second, (), 0, FRONTS)
    return jnp.where(jnp.arange(FRONTS) == fullest, PMAX, counts).astype(jnp.int32)


def draw_border_map(key, part):
    key = jax.random.fold_in(key, 23)
    block_rows = BORDER // N_COL
    root_rows = ROOT // N_COL
    keys = jax.random.split(key, FRONTS * N_COL)
    picks = jax.vmap(lambda k: jax.random.permutation(k, root_rows)[:block_rows])(keys)
    picks = picks.reshape(FRONTS, N_COL, block_rows)
    offsets = (jnp.arange(N_COL, dtype=jnp.int32) * root_rows)[None, :, None]
    return (picks + offsets).reshape(FRONTS, BORDER).astype(jnp.int32)


def shard_levels(rng, shape, cuts, low, top_value):
    factor_of = 1.0
    for axis_at, parts in cuts:
        draws = jax.random.uniform(jax.random.fold_in(jax.random.fold_in(rng, 6), axis_at), (parts,), jnp.float32, low / len(cuts), top_value / len(cuts))
        factor_of = factor_of * jnp.repeat(jnp.exp(draws), shape[axis_at] // parts).reshape((-1,) + (1,) * (len(shape) - 1 - axis_at))
    return factor_of


def gaussian(stream_key, shape, width, limit, pieces=(), kind=jnp.bfloat16):
    factor_of = shard_levels(stream_key, shape, pieces, -0.22, 0.18) if pieces else 1.0
    array = jax.random.normal(stream_key, shape, jnp.float32) * width * factor_of
    return jnp.minimum(jnp.maximum(array, -limit), limit).astype(kind)


def setup_inputs(seed: int = 0) -> dict:
    key_of = jax.random.split(jax.random.key(seed), 8)
    return {
        "child_rhs": gaussian(key_of[0], (FRONTS, PMAX, NRHS), 1.0, 6.0, ((0, 4), (1, 16)), jnp.float32),
        "root_rhs": gaussian(key_of[1], (ROOT, NRHS), 1.0, 6.0, ((0, 16),), jnp.float32),
        "child_inv": gaussian(key_of[2], (FRONTS, PMAX, PMAX), PMAX ** -0.5, 0.0625, ((0, 4), (1, 4), (2, 16)), jnp.float32),
        "coupling": gaussian(key_of[3], (FRONTS, PMAX, BORDER), PMAX ** -0.5, 0.0625, ((0, 4), (1, 4), (2, 16)), jnp.float32),
        "root_inv": gaussian(key_of[4], (ROOT, ROOT), ROOT ** -0.5, 0.0546875, ((0, 16), (1, 16)), jnp.float32),
        "pivot_counts": draw_pivot_counts(jax.random.fold_in(key_of[7], 71), 0),
        "border_map": draw_border_map(jax.random.fold_in(key_of[7], 71), 0),
    }


HIGH = lax.Precision.HIGHEST


def reference(child_rhs, root_rhs, child_inv, coupling, root_inv, pivot_counts, border_map):
    positions = jnp.arange(PMAX, dtype=jnp.int32)
    update = root_rhs
    forwards = []
    lives = []
    for front_id in range(FRONTS):
        live = (positions < pivot_counts[front_id]).astype(jnp.float32)[:, None]
        forward = live * jnp.dot(child_inv[front_id], live * child_rhs[front_id], precision=HIGH)
        border = jnp.dot(coupling[front_id].T, forward, precision=HIGH)
        update = update.at[border_map[front_id]].add(-border)
        forwards.append(forward)
        lives.append(live)
    root_forward = jnp.dot(root_inv, update, precision=HIGH)
    root_solution = jnp.dot(root_inv.T, root_forward, precision=HIGH)
    results = []
    for front_id in range(FRONTS):
        picked = root_solution[border_map[front_id]]
        reduced = lives[front_id] * (forwards[front_id] - jnp.dot(coupling[front_id], picked, precision=HIGH))
        results.append(lives[front_id] * jnp.dot(child_inv[front_id].T, reduced, precision=HIGH))
    return jnp.stack(results), root_solution
```

```python
import jax
import jax.numpy as jnp
from jax import lax
from jax.experimental import pallas as pl
from jax.experimental.pallas import tpu as pltpu
from jax.sharding import PartitionSpec as P

MESH = pl.DeviceIdType.MESH
F32 = jnp.float32
BF16 = jnp.bfloat16
NZ = 8
NXY = 16
BLK = 128
RBLK = 48
SLAB = 8
YSLAB = 32


def split(value):
    high = value.astype(BF16)
    low = (value - high.astype(F32)).astype(BF16)
    return high, low


def stack(value, axis):
    return jnp.concatenate(split(value), axis=axis)


def mm(left, right):
    return jnp.dot(left, right, preferred_element_type=F32)


def fold(value):
    rows, cols = value.shape[0] // 2, value.shape[1] // 2
    return (value[:rows, :cols] + value[:rows, cols:]) + (value[rows:, :cols] + value[rows:, cols:])


def halves(value):
    rows = value.shape[0] // 2
    return value[:rows] + value[rows:]


def far_first(step):
    return 4 + (1 - 2 * (step % 2)) * ((step + 1) // 2)


def plane_step(step):
    at = step + (step + 5) // 15 if isinstance(step, int) else step + (step + 5) // 15
    return (2 + at // 4) % 4, (2 + at % 4) % 4


def kernel(
    rhs_hbm, root_hbm, inv_hbm, cpl_hbm, rinv_hbm, counts, map_ref,
    child_out, root_out,
    rhs_v, root_v, inv_v, cpl_v, rinv_v,
    inv_hi, inv_lo, cpl_hi, cpl_lo, rin_hi, rin_lo,
    vec_hl, place, place_t, root_t,
    part1, core1, rs1, full1,
    part5, core5, rs5, full5,
    spread_s, xyr2, upd_t,
    part3, core3, rs3, full3,
    back_s, xyr4, back_t,
    pick_hl, acc_b, acc_c, own_fwd,
    ypart, yrs, yfull,
    load_sem, out_sem,
    c1s, c1r, z1s, z1r, g1s, g1r, s1s, s1r,
    c5s, c5r, z5s, z5r, g5s, g5r, s5s, s5r,
    c3s, c3r, z3s, z3r, g3s, g3r, s3s, s3r,
    p2s, p2r, q2s, q2r, p4s, p4r, q4s, q4r,
    y6s, y6r, w6s, w6r,
):
    f = lax.axis_index("front")
    r = lax.axis_index("row")
    c = lax.axis_index("col")
    z = c // 2
    k = c % 2
    sib = (f, r, z * 2 + (1 - k))

    def zdev(d):
        return (f, r, ((z + d) % NZ) * 2 + k)

    def xydev(df, dr):
        return ((f + df) % 4, (r + dr) % 4, c)

    def rcopy(src, dst, ss, rs, dev):
        return pltpu.make_async_remote_copy(
            src_ref=src, dst_ref=dst, send_sem=ss, recv_sem=rs, device_id=dev, device_id_type=MESH
        )

    def loop(n, body):
        def step(i, carry):
            body(i)
            return carry

        lax.fori_loop(0, n, step, 0)

    barrier = pltpu.get_barrier_semaphore()
    pl.semaphore_signal(barrier, inc=1, device_id=sib, device_id_type=MESH)
    for d in range(1, NZ):
        pl.semaphore_signal(barrier, inc=1, device_id=zdev(d), device_id_type=MESH)
    for e in range(1, NXY):
        pl.semaphore_signal(barrier, inc=1, device_id=xydev(e // 4, e % 4), device_id_type=MESH)

    def block_of(step):
        half = jnp.where(step < 8, 1 - k, k)
        return half * 8 + (z + far_first(step % 8)) % NZ

    def rows(block, size=BLK):
        return pl.ds(pl.multiple_of(block * size, size), size)

    def inv_load(step):
        at = rows(block_of(step))
        return pltpu.make_async_copy(inv_hbm.at[0, at], inv_v.at[at], load_sem.at[step])

    rhs_load = pltpu.make_async_copy(rhs_hbm.at[0], rhs_v, load_sem.at[16])
    cpl_load = pltpu.make_async_copy(cpl_hbm.at[0], cpl_v, load_sem.at[17])
    rinv_load = pltpu.make_async_copy(rinv_hbm, rinv_v, load_sem.at[18])
    root_load = pltpu.make_async_copy(root_hbm, root_v, load_sem.at[19])
    rhs_load.start()
    loop(16, lambda i: inv_load(i).start())
    cpl_load.start()
    rinv_load.start()
    root_load.start()

    count = counts[f]
    rhs_load.wait()
    spot = c * 512 + lax.broadcasted_iota(jnp.int32, (512, BLK), 0)
    vec_hl[...] = stack(jnp.where(spot < count, rhs_v[...], 0.0), 1)

    own = k * 8 + z

    def reduce_over_col(make, part, core, rs, cs, cr, zs, zr):
        def core_copy(step):
            at = rows(block_of(step))
            return rcopy(part.at[at], core.at[rows((z + far_first(step)) % NZ)], cs.at[step], cr.at[step], sib)

        def z_copy(step):
            at = rows(k * 8 + (z + far_first(step)) % NZ)
            return rcopy(part.at[at], rs.at[step], zs.at[step], zr.at[step], zdev(far_first(step)))

        def other(step):
            at = rows(block_of(step))
            part[at, :] = make(step, at)
            core_copy(step).start()

        def mine(step):
            at = rows(block_of(step + 8))
            value = make(step + 8, at)
            core_copy(step).wait_recv()
            part[at, :] = value + core[rows((z + far_first(step)) % NZ), :]

        def mine_send(step):
            mine(step)
            z_copy(step).start()

        loop(8, other)
        loop(7, mine_send)
        mine(7)

        def finish():
            total = part[rows(own), :]
            for step in range(7):
                z_copy(step).wait_recv()
                total = total + rs[step]
            return total

        def drain():
            loop(8, lambda i: core_copy(i).wait_send())
            loop(7, lambda i: z_copy(i).wait_send())

        return finish, drain

    def gather_over_col(full, size, gs, gr, ss, sr, use):
        def z_copy(step):
            at = rows(own, size)
            return rcopy(full.at[at], full.at[at], gs.at[step], gr.at[step], zdev(far_first(step)))

        def sib_copy(step):
            at = rows(k * 8 + (z + far_first(step)) % NZ, size)
            return rcopy(full.at[at], full.at[at], ss.at[step], sr.at[step], sib)

        def z_arrived(step):
            return (8 - far_first(step)) % NZ

        loop(7, lambda i: z_copy(i).start())
        sib_copy(7).start()
        use(own)

        def mine(i):
            step = 6 - i
            z_copy(step).wait_recv()
            d = z_arrived(step)
            at = rows(k * 8 + (z + d) % NZ, size)
            rcopy(full.at[at], full.at[at], ss.at[step], sr.at[step], sib).start()
            use(k * 8 + (z + d) % NZ)

        loop(7, mine)

        def other(i):
            step = 7 - i
            sib_copy(step).wait_recv()
            use((1 - k) * 8 + (z + z_arrived(step)) % NZ)

        loop(8, other)

        def drain():
            loop(7, lambda i: z_copy(i).wait_send())
            loop(8, lambda i: sib_copy(i).wait_send())

        return drain

    def sum_over_plane(src, recv, full, ps, pr, qs, qr, combine):
        me = f * 4 + r

        def slab(df, dr):
            return pl.ds(pl.multiple_of((((f + df) % 4) * 4 + (r + dr) % 4) * SLAB, SLAB), SLAB)

        def out_copy(step):
            df, dr = plane_step(step)
            return rcopy(src.at[slab(df, dr)], recv.at[step], ps.at[step], pr.at[step], xydev(df, dr))

        mine = pl.ds(pl.multiple_of(me * SLAB, SLAB), SLAB)

        def all_copy(step):
            df, dr = plane_step(step)
            return rcopy(full.at[mine], full.at[mine], qs.at[step], qr.at[step], xydev(df, dr))

        loop(15, lambda i: out_copy(i).start())
        total = src[mine, :]
        for step in range(15):
            out_copy(step).wait_recv()
            total = total + recv[step]
        full[mine, :] = combine(total, mine)
        loop(15, lambda i: all_copy(i).start())
        loop(15, lambda i: all_copy(i).wait_recv())

        def drain():
            loop(15, lambda i: out_copy(i).wait_send())
            loop(15, lambda i: all_copy(i).wait_send())

        return drain

    def make_forward(step, at):
        inv_load(step).wait()
        high, low = split(inv_v[at, :])
        inv_hi[at, :] = high
        inv_lo[at, :] = low
        return fold(mm(jnp.concatenate([high, low], axis=0), vec_hl[...]))

    pl.semaphore_wait(barrier, NZ + NXY - 1)
    finish1, drain1 = reduce_over_col(make_forward, part1, core1, rs1, c1s, c1r, z1s, z1r)

    cpl_load.wait()

    def split_cpl(i):
        at = rows(i)
        high, low = split(cpl_v[at, :])
        cpl_hi[at, :] = high
        cpl_lo[at, :] = low

    loop(16, split_cpl)
    rinv_load.wait()

    def split_rinv(i):
        at = rows(i)
        high, low = split(rinv_v[at, :])
        rin_hi[at, :] = high
        rin_lo[at, :] = low

    loop(6, split_rinv)

    def build_map(i):
        at = rows(i)
        spots = i * BLK + lax.broadcasted_iota(jnp.int32, (BLK, 384), 0)
        hot = (map_ref[...] - c * 768 == spots).astype(F32)
        place[at, :] = hot.astype(BF16)
        place_t[i] = hot.T.astype(BF16)

    loop(6, build_map)
    root_load.wait()
    for i in range(6):
        root_t[:, i * BLK:(i + 1) * BLK] = root_v[i * BLK:(i + 1) * BLK, :].T

    live_at = r * 2048 + own * BLK + lax.broadcasted_iota(jnp.int32, (BLK, BLK), 0)
    forward = jnp.where(live_at < count, finish1(), 0.0)
    own_fwd[...] = forward
    full1[rows(own), :] = forward
    acc_b[...] = jnp.zeros_like(acc_b)

    def use_border(block):
        at = rows(block)
        left = stack(full1[at, :].T, 0)
        acc_b[:, :384] += mm(left, cpl_hi[at, :])
        acc_b[:, 384:] += mm(left, cpl_lo[at, :])

    drain2 = gather_over_col(full1, BLK, g1s, g1r, s1s, s1r, use_border)
    border_hl = stack(fold(acc_b[...]), 0)
    for i in range(6):
        spread_s[:, i * BLK:(i + 1) * BLK] = halves(mm(border_hl, place_t[i]))
    drain3 = sum_over_plane(
        spread_s, xyr2, upd_t, p2s, p2r, q2s, q2r, lambda total, mine: root_t[mine, :] - total
    )

    upd_hl = jnp.concatenate([stack(upd_t[:, i * BLK:(i + 1) * BLK].T, 1) for i in range(6)], axis=0)

    def root_rows(i):
        at = rows(i)
        part3[at, :] = fold(mm(jnp.concatenate([rin_hi[at, :], rin_lo[at, :]], axis=0), upd_hl))

    loop(3, lambda i: root_rows((1 - k) * 3 + i))
    half_other = pl.ds(pl.multiple_of((1 - k) * 384, 384), 384)
    half_mine = pl.ds(pl.multiple_of(k * 384, 384), 384)
    core_copy3 = rcopy(part3.at[half_other], core3, c3s.at[0], c3r.at[0], sib)
    core_copy3.start()
    loop(3, lambda i: root_rows(k * 3 + i))
    core_copy3.wait_recv()
    part3[half_mine, :] += core3[...]

    def z_copy3(step):
        at = rows(k * 8 + (z + far_first(step)) % NZ, RBLK)
        return rcopy(part3.at[at], rs3.at[step], z3s.at[step], z3r.at[step], zdev(far_first(step)))

    loop(7, lambda i: z_copy3(i).start())
    total = part3[rows(own, RBLK), :]
    for step in range(7):
        z_copy3(step).wait_recv()
        total = total + rs3[step]
    full3[rows(own, RBLK), :] = total
    drain4 = gather_over_col(full3, RBLK, g3s, g3r, s3s, s3r, lambda block: None)

    fwd_hl = jnp.concatenate([stack(full3[i * BLK:(i + 1) * BLK, :].T, 0) for i in range(6)], axis=1)
    back_s[...] = halves(mm(fwd_hl, rin_hi[...]) + mm(fwd_hl, rin_lo[...]))
    drain5 = sum_over_plane(back_s, xyr4, back_t, p4s, p4r, q4s, q4r, lambda total, mine: total)
    pick = halves(mm(stack(back_t[...], 0), place[...]))
    for i in range(3):
        pick_hl[i * BLK:(i + 1) * BLK, :] = stack(pick[:, i * BLK:(i + 1) * BLK].T, 1)

    def make_correction(step, at):
        return fold(mm(jnp.concatenate([cpl_hi[at, :], cpl_lo[at, :]], axis=0), pick_hl[...]))

    finish5, drain6 = reduce_over_col(make_correction, part5, core5, rs5, c5s, c5r, z5s, z5r)
    for i in range(6):
        root_v[i * BLK:(i + 1) * BLK, :] = back_t[:, i * BLK:(i + 1) * BLK].T
    root_store = pltpu.make_async_copy(root_v, root_out, out_sem.at[0])
    root_store.start()
    full5[rows(own), :] = jnp.where(live_at < count, own_fwd[...] - finish5(), 0.0)
    acc_c[...] = jnp.zeros_like(acc_c)

    def use_back(block):
        at = rows(block)
        left = stack(full5[at, :].T, 0)
        acc_c[...] += mm(left, inv_hi[at, :]) + mm(left, inv_lo[at, :])

    drain7 = gather_over_col(full5, BLK, g5s, g5r, s5s, s5r, use_back)
    ypart[...] = halves(acc_c[...])

    def yslab(d):
        return pl.ds(pl.multiple_of(((r + d) % 4) * YSLAB, YSLAB), YSLAB)

    def ydev(d):
        return (f, (r + d) % 4, c)

    def y_copy(d):
        return rcopy(ypart.at[yslab(d)], yrs.at[d - 1], y6s.at[d - 1], y6r.at[d - 1], ydev(d))

    def w_copy(d):
        return rcopy(yfull.at[yslab(0)], yfull.at[yslab(0)], w6s.at[d - 1], w6r.at[d - 1], ydev(d))

    for d in (2, 1, 3):
        y_copy(d).start()
    total = ypart[yslab(0), :]
    for d in (1, 3, 2):
        y_copy(d).wait_recv()
        total = total + yrs[d - 1]
    yfull[yslab(0), :] = total
    for d in (2, 1, 3):
        w_copy(d).start()
    for d in (1, 3, 2):
        w_copy(d).wait_recv()
    for i in range(4):
        at = c * 512 + i * BLK + lax.broadcasted_iota(jnp.int32, (BLK, BLK), 0)
        rhs_v[i * BLK:(i + 1) * BLK, :] = jnp.where(at < count, yfull[:, i * BLK:(i + 1) * BLK].T, 0.0)
    child_store = pltpu.make_async_copy(rhs_v, child_out.at[0], out_sem.at[1])
    child_store.start()

    drain1()
    drain2()
    drain3()
    core_copy3.wait_send()
    loop(7, lambda i: z_copy3(i).wait_send())
    drain4()
    drain5()
    drain6()
    drain7()
    for d in (1, 2, 3):
        y_copy(d).wait_send()
        w_copy(d).wait_send()
    root_store.wait()
    child_store.wait()


def per_device(child_rhs, root_rhs, child_inv, coupling, root_inv, pivot_counts, border_map):
    v = pltpu.VMEM
    dma = pltpu.SemaphoreType.DMA
    col_sems = [dma((8,))] * 8
    scratch = [
        v((512, 128), F32), v((768, 128), F32), v((2048, 512), F32), v((2048, 384), F32), v((768, 768), F32),
        v((2048, 512), BF16), v((2048, 512), BF16), v((2048, 384), BF16), v((2048, 384), BF16),
        v((768, 768), BF16), v((768, 768), BF16),
        v((512, 256), BF16), v((768, 384), BF16), v((6, 384, 128), BF16), v((128, 768), F32),
        v((2048, 128), F32), v((1024, 128), F32), v((7, 128, 128), F32), v((2048, 128), F32),
        v((2048, 128), F32), v((1024, 128), F32), v((7, 128, 128), F32), v((2048, 128), F32),
        v((128, 768), F32), v((15, 8, 768), F32), v((128, 768), F32),
        v((768, 128), F32), v((384, 128), F32), v((7, 48, 128), F32), v((768, 128), F32),
        v((128, 768), F32), v((15, 8, 768), F32), v((128, 768), F32),
        v((384, 256), BF16), v((256, 768), F32), v((256, 512), F32), v((128, 128), F32),
        v((128, 512), F32), v((3, 32, 512), F32), v((128, 512), F32),
        dma((20,)), dma((2,)),
    ] + col_sems * 3 + [dma((15,))] * 8 + [dma((3,))] * 4
    hbm = pl.BlockSpec(memory_space=pl.ANY)
    return tuple(
        pl.pallas_call(
            kernel,
            out_shape=(
                jax.ShapeDtypeStruct((1, 512, 128), F32),
                jax.ShapeDtypeStruct((768, 128), F32),
            ),
            in_specs=[hbm] * 5
            + [pl.BlockSpec(memory_space=pltpu.SMEM), pl.BlockSpec(memory_space=pltpu.VMEM)],
            out_specs=(hbm, hbm),
            scratch_shapes=scratch,
            compiler_params=pltpu.CompilerParams(
                collective_id=0, has_side_effects=True, vmem_limit_bytes=56 << 20
            ),
            cost_estimate=pl.CostEstimate(flops=5 * 10**9, bytes_accessed=11 * 10**6, transcendentals=0),
        )(child_rhs, root_rhs, child_inv, coupling, root_inv, pivot_counts, border_map)
    )


def solution(mesh):
    in_specs = (
        P("front", "col", None),
        P("col", None),
        P("front", "row", "col"),
        P("front", "row", "col"),
        P(("front", "row"), "col"),
        P(),
        P("front", "col"),
    )
    out_specs = (P("front", "col", None), P("col", None))
    return jax.shard_map(
        per_device, mesh=mesh, in_specs=in_specs, out_specs=out_specs, check_vma=False
    )
```

```python
import jax
import jax.numpy as jnp
from jax import lax
from jax.experimental import pallas as pl
from jax.experimental.pallas import tpu as pltpu
from jax.sharding import PartitionSpec as P

MESH = pl.DeviceIdType.MESH
F32 = jnp.float32
BF16 = jnp.bfloat16
NZ = 8
NXY = 16
BLK = 128
SRC = 64


def split(value):
    high = value.astype(BF16)
    low = (value - high.astype(F32)).astype(BF16)
    return high, low


def stack(value):
    return jnp.concatenate(split(value), axis=0)


def mm(left, right):
    return jnp.dot(left, right, preferred_element_type=F32)


def nt(left, right):
    return lax.dot_general(left, right, (((1,), (1,)), ((), ())), preferred_element_type=F32)


def halves(value):
    rows = value.shape[0] // 2
    return value[:rows] + value[rows:]


def join(left, right, axis):
    return jnp.concatenate([left, right], axis=axis)


def far_first(step):
    return 4 + (1 - 2 * (step % 2)) * ((step + 1) // 2)


def plane_step(step):
    at = step + (step + 5) // 15
    return (2 + at // 4) % 4, (2 + at % 4) % 4


def gather_offset(at):
    size = jnp.where(at < 1, 0, jnp.where(at < 3, 2, jnp.where(at < 5, 1, jnp.where(at < 7, 3, 4))))
    return size * (1 - 2 * (at % 2))


def loop(n, body):
    def step(i, carry):
        body(i)
        return carry

    lax.fori_loop(0, n, step, 0)


def rows(block, size=BLK):
    return pl.ds(pl.multiple_of(block * size, size), size)


def kernel(
    rhs_hbm, root_hbm, inv_hbm, cpl_hbm, rinv_hbm, counts, map_ref,
    child_out, root_out,
    rhs_v, root_v, inv_v, cpl_v, rinv_v,
    inv_hi, inv_lo, cpl_hi, cpl_lo, rin_hi, rin_lo,
    vec_hl, place, root_t, fwd,
    part1, core1, rs1, full1,
    part5, core5, rs5, full5,
    spread_s, xyr2, upd_t,
    part3, core3, rs3, full3,
    back_s, xyr4, back_t,
    pick_hl, acc_b, acc_c,
    ypart, yrs, yfull,
    load_sem, out_sem,
    c1s, z1s, g1s, p2s, c3s, z3s, g3s, p4s, c5s, z5s, g5s, y6s,
    c1r, z1r, g1r, s1r, c3r, z3r, g3r, s3r, c5r, z5r, g5r, s5r,
    p2r, q2r, p4r, q4r, y6r, w6r,
):
    f = lax.axis_index("front")
    r = lax.axis_index("row")
    c = lax.axis_index("col")
    z = c // 2
    k = c % 2
    sib = (f, r, z * 2 + (1 - k))

    way = 1 - 2 * k

    def chip(d):
        return (z + way * d + 2 * NZ) % NZ

    def zdev(d):
        return (f, r, chip(d) * 2 + k)

    def xydev(df, dr):
        return ((f + df) % 4, (r + dr) % 4, c)

    def rcopy(src, dst, ss, rs, dev):
        return pltpu.make_async_remote_copy(
            src_ref=src, dst_ref=dst, send_sem=ss, recv_sem=rs, device_id=dev, device_id_type=MESH
        )

    def await_blocks(sem, count):
        at = inv_v.at[pl.ds(0, count * 16)]
        pltpu.make_async_copy(at, at, sem).wait()

    def await_slabs(sem, count):
        at = cpl_v.at[pl.ds(0, count * 8)]
        pltpu.make_async_copy(at, at, sem).wait()

    barrier = pltpu.get_barrier_semaphore()
    pl.semaphore_signal(barrier, inc=1, device_id=sib, device_id_type=MESH)
    for d in (-2, -1, 1, 2):
        pl.semaphore_signal(barrier, inc=1, device_id=zdev(d), device_id_type=MESH)
    for e in range(1, NXY):
        pl.semaphore_signal(barrier, inc=1, device_id=xydev(e // 4, e % 4), device_id_type=MESH)

    def zat(step):
        return chip(far_first(step))

    def block_of(step):
        side = jnp.where(step < 8, -1, 1)
        half = jnp.where(step < 8, 1 - k, k)
        return half * 8 + chip(side * far_first(step % 8))

    def zat_other(step):
        return chip(-far_first(step))

    def inv_load(step):
        at = rows(block_of(step))
        return pltpu.make_async_copy(inv_hbm.at[0, at], inv_v.at[at], load_sem.at[step])

    rhs_load = pltpu.make_async_copy(rhs_hbm.at[0], rhs_v, load_sem.at[16])
    cpl_load = pltpu.make_async_copy(cpl_hbm.at[0], cpl_v, load_sem.at[17])
    rinv_load = pltpu.make_async_copy(rinv_hbm, rinv_v, load_sem.at[18])
    root_load = pltpu.make_async_copy(root_hbm, root_v, load_sem.at[19])
    rhs_load.start()
    loop(16, lambda i: inv_load(i).start())
    cpl_load.start()
    rinv_load.start()
    root_load.start()

    count = counts[f]
    own = k * 8 + z
    rhs_load.wait()
    for i in range(4):
        spot = c * 512 + i * BLK + lax.broadcasted_iota(jnp.int32, (BLK, BLK), 1)
        high, low = split(jnp.where(spot < count, rhs_v[i * BLK:(i + 1) * BLK, :].T, 0.0))
        vec_hl[:BLK, i * BLK:(i + 1) * BLK] = high
        vec_hl[BLK:, i * BLK:(i + 1) * BLK] = low


    def pair_at(pair):
        return rows(block_of(2 * pair)), rows(block_of(2 * pair + 1))

    def z_reduce(part, rs, zs, zr):
        def copy(index, src, d):
            return rcopy(src, rs.at[index], zs, zr.at[(0, 0, 1, 2, 2, 2, 2)[index]], zdev(d))

        def send(step):
            index = {0: 0, 1: 1, 2: 2, 5: 3, 6: 4}[step]
            return copy(index, part(zat(step)), {0: 2, 1: 1, 2: -1, 5: 1, 6: -1}[step])

        def arrived(begin, end, sem):
            at = rs.at[pl.ds(begin, end - begin)]
            pltpu.make_async_copy(at, at, zr.at[sem]).wait()

        def relay():
            arrived(0, 2, 0)
            part(chip(2))[...] += rs[0] + rs[1]
            copy(5, part(chip(2)), 2).start()
            arrived(2, 3, 1)
            part(chip(-2))[...] += rs[2]
            copy(6, part(chip(-2)), -2).start()

        def total():
            arrived(3, 7, 2)
            return part(z)[...] + ((rs[3] + rs[4]) + (rs[5] + rs[6]))

        return send, relay, total

    def gather(piece, gs, gr, sr):
        def z_copy(index, d_owner, d):
            at = piece(k, chip(d_owner))
            return rcopy(at, at, gs, gr.at[index], zdev(d))

        def sib_copy(owner):
            at = piece(k, owner)
            return rcopy(at, at, gs, sr.at[owner], sib)

        def sib_arrival(owner):
            at = piece(1 - k, owner)
            return rcopy(at, at, gs, sr.at[owner], sib)

        first = [(0, 0, 2), (1, 0, -2), (2, 0, 1), (3, 0, -1)]
        second = [(4, -2, 1), (5, -2, 2), (6, 2, -1)]
        arrivals = {0: -2, 1: 2, 2: -1, 3: 1, 4: -3, 5: -4, 6: 3}

        def arrive(index):
            z_copy(index, arrivals[index], 1).wait_recv()
            sib_copy(chip(arrivals[index])).start()

        def start():
            for item in first:
                z_copy(*item).start()
            sib_copy(z).start()

        def near():
            arrive(0)
            z_copy(*second[0]).start()
            z_copy(*second[1]).start()
            arrive(1)
            z_copy(*second[2]).start()
            arrive(2)
            arrive(3)

        def far():
            arrive(6)
            arrive(4)
            arrive(5)

        def take(begin, end, use):
            def body(i):
                owner = chip(gather_offset(i + begin))
                sib_arrival(owner).wait_recv()
                use(owner)

            loop(end - begin, body)

        return start, near, far, take


    def slab(p):
        return p % 2, rows(p // 2, 8)

    def plane_at(df, dr):
        return slab(((f + df) % 4) * 4 + (r + dr) % 4)

    here = plane_at(0, 0)

    def plane(src, recv, full, ps, pr, qr):
        def out_copy(step):
            df, dr = plane_step(step)
            return rcopy(src.at[plane_at(df, dr)], recv.at[step], ps, pr, xydev(df, dr))

        def all_copy(step):
            df, dr = plane_step(step)
            return rcopy(full.at[here], full.at[here], ps, qr, xydev(df, dr))

        def start():
            loop(15, lambda i: out_copy(i).start())

        def middle(combine):
            total = src[here]
            pltpu.make_async_copy(recv, recv, pr).wait()
            for step in range(15):
                total = total + recv[step]
            full[here] = combine(total)
            loop(15, lambda i: all_copy(i).start())

        def finish():
            await_slabs(qr, 15)
            return join(full[0], full[1], 1)

        return start, middle, finish


    def forward_pair(pair):
        sides = []
        for step in (2 * pair, 2 * pair + 1):
            inv_load(step).wait()
            at = rows(block_of(step))
            high, low = split(inv_v[at, :])
            inv_hi[at, :] = high
            inv_lo[at, :] = low
            sides.append((high, low))
        (high1, low1), (high2, low2) = sides
        value = halves(nt(vec_hl[...], join(high1, high2, 0)) + nt(vec_hl[...], join(low1, low2, 0)))
        return value[:, :BLK], value[:, BLK:]

    def core_copy1(step):
        return rcopy(part1.at[block_of(step)], core1.at[zat_other(step)], c1s, c1r.at[step], sib)

    def other1(pair):
        first, second = forward_pair(pair)
        part1[block_of(2 * pair)] = first
        part1[block_of(2 * pair + 1)] = second

    loop(4, other1)
    pl.semaphore_wait(barrier, NXY + 4)
    loop(8, lambda i: core_copy1(i).start())

    src_rows = [pl.ds(0, SRC), pl.ds(SRC, SRC)]
    sum1 = [
        z_reduce(lambda owner, h=h: part1.at[k * 8 + owner, src_rows[h]], rs1.at[h], z1s, z1r.at[h])
        for h in range(2)
    ]
    for pair in range(4):
        values = forward_pair(pair + 4)
        for j in range(2):
            step = 2 * pair + j
            core_copy1(step).wait_recv()
            part1[k * 8 + zat(step)] = values[j] + core1[zat(step)]
            if step in (0, 1, 2, 5, 6):
                sum1[0][0](step).start()
    for step in (0, 1, 2, 5, 6):
        sum1[1][0](step).start()

    cpl_load.wait()

    def split_cpl(i):
        at = rows(i)
        high, low = split(cpl_v[at, :])
        cpl_hi[at, :] = high
        cpl_lo[at, :] = low

    loop(16, split_cpl)
    rinv_load.wait()

    def split_rinv(i):
        at = rows(i)
        high, low = split(rinv_v[at, :])
        rin_hi[at, :] = high
        rin_lo[at, :] = low

    loop(6, split_rinv)

    def build_map(i):
        at = rows(i)
        spots = i * BLK + lax.broadcasted_iota(jnp.int32, (BLK, 384), 0)
        place[at, :] = (map_ref[...] - c * 768 == spots).astype(F32).astype(BF16)

    loop(6, build_map)
    root_load.wait()
    for i in range(6):
        turned = root_v[i * BLK:(i + 1) * BLK, :].T
        for h in range(2):
            root_t[h, i // 3, :, (i % 3) * BLK:(i % 3 + 1) * BLK] = turned[h * SRC:(h + 1) * SRC]
    acc_b[...] = jnp.zeros_like(acc_b)
    acc_c[...] = jnp.zeros_like(acc_c)
    live = r * 2048 + own * BLK + lax.broadcasted_iota(jnp.int32, (SRC, BLK), 1) < count

    ag1, xy2, ag3, xy4, ag5 = [], [], [], [], []
    for h in range(2):
        sum1[h][1]()
    for h in range(2):
        forward = jnp.where(live, sum1[h][2](), 0.0)
        fwd[h] = forward
        full1[h, own] = forward
        ag1.append(gather(lambda kk, zz, h=h: full1.at[h, kk * 8 + zz], g1s, g1r.at[h], s1r.at[h]))
        ag1[h][0]()

    def use_border(h):
        def use(owner):
            left = stack(join(full1[h, k * 8 + owner], full1[h, (1 - k) * 8 + owner], 1))
            mine, other = rows(k * 8 + owner), rows((1 - k) * 8 + owner)
            acc_b[h] += mm(left, join(cpl_hi[mine, :], cpl_hi[other, :], 0)) + mm(
                left, join(cpl_lo[mine, :], cpl_lo[other, :], 0)
            )

        return use

    ag1[0][1]()
    ag1[0][3](0, 4, use_border(0))
    ag1[1][1]()
    for h in range(2):
        if h:
            ag1[h][3](0, 4, use_border(h))
        ag1[h][2]()
        ag1[h][3](4, 8, use_border(h))
        border_hl = stack(halves(acc_b[h]))
        for half in range(2):
            spread_s[h, half] = halves(nt(border_hl, place[half * 384:(half + 1) * 384, :]))
        xy2.append(plane(
            spread_s.at[h], xyr2.at[h], upd_t.at[h], p2s, p2r.at[h], q2r.at[h]
        ))
        xy2[h][0]()

    for h in range(2):
        xy2[h][1](lambda total, h=h: root_t.at[h][here] - total)

    def core_copy3(h):
        return rcopy(
            part3.at[h, :, rows(1 - k, 32)], core3.at[h], c3s, c3r.at[h], sib
        )

    def slab3(kk, zz):
        return zz % 2, rows(kk * 4 + zz // 2, 8)

    for h in range(2):
        upd_hl = stack(xy2[h][2]())
        value = halves(nt(upd_hl, rin_hi[...]) + nt(upd_hl, rin_lo[...]))
        part3[h, 0] = value[:, :384]
        part3[h, 1] = value[:, 384:]
        core_copy3(h).start()
    sum3 = []
    for h in range(2):
        core_copy3(h).wait_recv()
        part3[h, :, rows(k, 32)] += core3[h]
        sum3.append(z_reduce(
            lambda owner, h=h: part3.at[h].at[slab3(k, owner)], rs3.at[h], z3s, z3r.at[h]
        ))
        for step in (0, 1, 2, 5, 6):
            sum3[h][0](step).start()
    for h in range(2):
        sum3[h][1]()
    for h in range(2):
        full3.at[h][slab3(k, z)] = sum3[h][2]()
        ag3.append(gather(lambda kk, zz, h=h: full3.at[h].at[slab3(kk, zz)], g3s, g3r.at[h], s3r.at[h]))
        ag3[h][0]()

    for h in range(2):
        ag3[h][1]()
    for h in range(2):
        ag3[h][2]()
        ag3[h][3](0, 8, lambda owner: None)
        fwd_hl = stack(join(full3[h, 0], full3[h, 1], 1))
        value = halves(mm(fwd_hl, rin_hi[...]) + mm(fwd_hl, rin_lo[...]))
        back_s[h, 0] = value[:, :384]
        back_s[h, 1] = value[:, 384:]
        xy4.append(plane(
            back_s.at[h], xyr4.at[h], back_t.at[h], p4s, p4r.at[h], q4r.at[h]
        ))
        xy4[h][0]()
    for h in range(2):
        xy4[h][1](lambda total: total)

    def core_copy5(h, step):
        return rcopy(part5.at[h, block_of(step)], core5.at[h, zat_other(step)], c5s, c5r.at[h, step], sib)

    sum5 = []
    for h in range(2):
        pick_hl[h] = stack(halves(mm(stack(xy4[h][2]()), place[...])))

        def correction_pair(pair, h=h):
            at1, at2 = pair_at(pair)
            left = pick_hl[h]
            value = halves(
                nt(left, join(cpl_hi[at1, :], cpl_hi[at2, :], 0)) + nt(left, join(cpl_lo[at1, :], cpl_lo[at2, :], 0))
            )
            return value[:, :BLK], value[:, BLK:]

        def other5(pair, h=h):
            values = correction_pair(pair)
            for j in range(2):
                part5[h, block_of(2 * pair + j)] = values[j]
                core_copy5(h, 2 * pair + j).start()

        sum5.append(z_reduce(
            lambda owner, h=h: part5.at[h, k * 8 + owner], rs5.at[h], z5s, z5r.at[h]
        ))
        loop(4, other5)
        if h:
            sum5[0][1]()
        for pair in range(4):
            values = correction_pair(pair + 4)
            for j in range(2):
                step = 2 * pair + j
                core_copy5(h, step).wait_recv()
                part5[h, k * 8 + zat(step)] = values[j] + core5[h, zat(step)]
                if step in (0, 1, 2, 5, 6):
                    sum5[h][0](step).start()

    for i in range(6):
        half, at = i // 3, (i % 3) * BLK
        root_v[i * BLK:(i + 1) * BLK, :] = join(back_t[0, half, :, at:at + BLK], back_t[1, half, :, at:at + BLK], 0).T
    root_store = pltpu.make_async_copy(root_v, root_out, out_sem.at[0])
    root_store.start()

    sum5[1][1]()
    for h in range(2):
        full5[h, own] = jnp.where(live, fwd[h] - sum5[h][2](), 0.0)
        ag5.append(gather(lambda kk, zz, h=h: full5.at[h, kk * 8 + zz], g5s, g5r.at[h], s5r.at[h]))
        ag5[h][0]()

    def yslab(d):
        return rows((r + d) % 4, 16)

    def ydev(d):
        return (f, (r + d) % 4, c)

    def y_copy(h, d):
        return rcopy(ypart.at[h, yslab(d)], yrs.at[h, d - 1], y6s, y6r.at[h], ydev(d))

    def w_copy(h, d):
        return rcopy(yfull.at[h, yslab(0)], yfull.at[h, yslab(0)], y6s, w6r.at[h], ydev(d))

    def use_back(h):
        def use(owner):
            left = stack(join(full5[h, k * 8 + owner], full5[h, (1 - k) * 8 + owner], 1))
            mine, other = rows(k * 8 + owner), rows((1 - k) * 8 + owner)
            acc_c[h] += mm(left, join(inv_hi[mine, :], inv_hi[other, :], 0)) + mm(
                left, join(inv_lo[mine, :], inv_lo[other, :], 0)
            )

        return use

    ag5[0][1]()
    ag5[0][3](0, 4, use_back(0))
    ag5[1][1]()
    for h in range(2):
        if h:
            ag5[h][3](0, 4, use_back(h))
        ag5[h][2]()
        ag5[h][3](4, 8, use_back(h))
        ypart[h] = halves(acc_c[h])
        for d in (2, 1, 3):
            y_copy(h, d).start()
    for h in range(2):
        total = ypart[h, yslab(0)]
        pltpu.make_async_copy(yrs.at[h], yrs.at[h], y6r.at[h]).wait()
        for d in (1, 3, 2):
            total = total + yrs[h, d - 1]
        yfull[h, yslab(0)] = total
        for d in (2, 1, 3):
            w_copy(h, d).start()
    for h in range(2):
        await_blocks(w6r.at[h], 3)
    for i in range(4):
        at = c * 512 + i * BLK + lax.broadcasted_iota(jnp.int32, (BLK, BLK), 0)
        value = join(yfull[0, :, i * BLK:(i + 1) * BLK], yfull[1, :, i * BLK:(i + 1) * BLK], 0).T
        rhs_v[i * BLK:(i + 1) * BLK, :] = jnp.where(at < count, value, 0.0)
    child_store = pltpu.make_async_copy(rhs_v, child_out.at[0], out_sem.at[1])
    child_store.start()
    await_blocks(c1s, 8 * 2)
    await_blocks(z1s, 2 * 7)
    await_blocks(g1s, 2 * 15)
    await_slabs(p2s, 2 * 30)
    await_slabs(c3s, 2 * 8)
    await_slabs(z3s, 2 * 7)
    await_slabs(g3s, 2 * 15)
    await_slabs(p4s, 2 * 30)
    await_blocks(c5s, 2 * 8)
    await_blocks(z5s, 2 * 7)
    await_blocks(g5s, 2 * 15)
    await_blocks(y6s, 2 * 6)
    root_store.wait()
    child_store.wait()


def hand_over(child, root, child_out, root_out):
    child_out[...] = child[...]
    root_out[...] = root[...]


def per_device(child_rhs, root_rhs, child_inv, coupling, root_inv, pivot_counts, border_map):
    def v(*shape, dtype=F32):
        return pltpu.VMEM(shape, dtype)

    dma = pltpu.SemaphoreType.DMA
    scratch = [
        v(512, 128), v(768, 128), v(2048, 512), v(2048, 384), v(768, 768),
        v(2048, 512, dtype=BF16), v(2048, 512, dtype=BF16), v(2048, 384, dtype=BF16), v(2048, 384, dtype=BF16),
        v(768, 768, dtype=BF16), v(768, 768, dtype=BF16),
        v(256, 512, dtype=BF16), v(768, 384, dtype=BF16), v(2, 2, 64, 384), v(2, 64, 128),
        v(16, 128, 128), v(8, 128, 128), v(2, 7, 64, 128), v(2, 16, 64, 128),
        v(2, 16, 64, 128), v(2, 8, 64, 128), v(2, 7, 64, 128), v(2, 16, 64, 128),
        v(2, 2, 64, 384), v(2, 15, 8, 384), v(2, 2, 64, 384),
        v(2, 2, 64, 384), v(2, 2, 32, 384), v(2, 7, 8, 384), v(2, 2, 64, 384),
        v(2, 2, 64, 384), v(2, 15, 8, 384), v(2, 2, 64, 384),
        v(2, 128, 384, dtype=BF16), v(2, 128, 384), v(2, 128, 512),
        v(2, 64, 512), v(2, 3, 16, 512), v(2, 64, 512),
        dma((20,)), dma((2,)),
    ]
    scratch += [dma] * 12
    scratch += [dma((8,)), dma((2, 3)), dma((2, 7)), dma((2, 8))]
    scratch += [dma((2,)), dma((2, 3)), dma((2, 7)), dma((2, 8))]
    scratch += [dma((2, 8)), dma((2, 3)), dma((2, 7)), dma((2, 8))]
    scratch += [dma((2,))] * 6
    hbm = pl.BlockSpec(memory_space=pl.ANY)
    results = tuple(
        pl.pallas_call(
            kernel,
            out_shape=(
                jax.ShapeDtypeStruct((1, 512, 128), F32),
                jax.ShapeDtypeStruct((768, 128), F32),
            ),
            in_specs=[hbm] * 5
            + [pl.BlockSpec(memory_space=pltpu.SMEM), pl.BlockSpec(memory_space=pltpu.VMEM)],
            out_specs=(hbm, hbm),
            scratch_shapes=scratch,
            compiler_params=pltpu.CompilerParams(
                collective_id=0, has_side_effects=True, vmem_limit_bytes=56 << 20
            ),
            cost_estimate=pl.CostEstimate(flops=5 * 10**9, bytes_accessed=11 * 10**6, transcendentals=0),
        )(child_rhs, root_rhs, child_inv, coupling, root_inv, pivot_counts, border_map)
    )
    vmem = pl.BlockSpec(memory_space=pltpu.VMEM)
    return tuple(
        pl.pallas_call(
            hand_over,
            out_shape=tuple(jax.ShapeDtypeStruct(a.shape, a.dtype) for a in results),
            in_specs=[vmem] * 2,
            out_specs=(vmem, vmem),
        )(*results)
    )


def solution(mesh):
    in_specs = (
        P("front", "col", None),
        P("col", None),
        P("front", "row", "col"),
        P("front", "row", "col"),
        P(("front", "row"), "col"),
        P(),
        P("front", "col"),
    )
    out_specs = (P("front", "col", None), P("col", None))
    return jax.shard_map(
        per_device, mesh=mesh, in_specs=in_specs, out_specs=out_specs, check_vma=False
    )
```

```python
import jax
import jax.numpy as jnp
from jax import lax
from jax.experimental import pallas as pl
from jax.experimental.pallas import tpu as pltpu
from jax.sharding import PartitionSpec as P

MESH = pl.DeviceIdType.MESH
F32 = jnp.float32
BF16 = jnp.bfloat16
NZ = 8
NXY = 16
BLK = 128
SRC = 64
ARRIVALS = (0, -2, 2, -1, 1, 3, -3, -4)


def split(value):
    high = value.astype(BF16)
    low = (value - high.astype(F32)).astype(BF16)
    return high, low


def stack(value):
    return jnp.concatenate(split(value), axis=0)


def mm(left, right):
    return jnp.dot(left, right, preferred_element_type=F32)


def halves(value):
    rows = value.shape[0] // 2
    return value[:rows] + value[rows:]


def join(left, right, axis):
    return jnp.concatenate([left, right], axis=axis)


def far_first(step):
    return 4 + (1 - 2 * (step % 2)) * ((step + 1) // 2)


def plane_step(step):
    at = step + (step + 5) // 15
    return (2 + at // 4) % 4, (2 + at % 4) % 4


def loop(n, body):
    def step(i, carry):
        body(i)
        return carry

    lax.fori_loop(0, n, step, 0)


def rows(block, size=BLK):
    return pl.ds(pl.multiple_of(block * size, size), size)


def kernel(
    rhs_hbm, root_hbm, inv_hbm, cpl_hbm, rinv_hbm, counts, map_ref,
    child_out, root_out,
    rhs_v, root_v, inv_v, cpl_v, rinv_v,
    inv_hi, inv_lo, cpl_hi, cpl_lo, rin_hi, rin_lo,
    vec_hl, place, place_t, cplt_hi, cplt_lo, rint_hi, rint_lo, root_t, fwd,
    part1, core1, rs1, full1,
    part5, core5, rs5, full5,
    spread_s, xyr2, upd_t,
    part3, core3, rs3, full3,
    back_s, xyr4, back_t,
    acc_b, acc_c,
    ypart, yrs, yfull,
    load_sem, out_sem,
    c1s, z1s, g1s, p2s, c3s, z3s, g3s, p4s, c5s, z5s, g5s, y6s,
    c1r, z1r, g1r, s1r, c3r, z3r, g3r, s3r, c5r, z5r, g5r, s5r,
    p2r, q2r, p4r, q4r, y6r, w6r,
):
    f = lax.axis_index("front")
    r = lax.axis_index("row")
    c = lax.axis_index("col")
    z = c // 2
    k = c % 2
    sib = (f, r, z * 2 + (1 - k))

    way = 1 - 2 * k

    def chip(d):
        return (z + way * d + 2 * NZ) % NZ

    def zdev(d):
        return (f, r, chip(d) * 2 + k)

    def xydev(df, dr):
        return ((f + df) % 4, (r + dr) % 4, c)

    def rcopy(src, dst, ss, rs, dev):
        return pltpu.make_async_remote_copy(
            src_ref=src, dst_ref=dst, send_sem=ss, recv_sem=rs, device_id=dev, device_id_type=MESH
        )

    def await_blocks(sem, count):
        at = inv_v.at[pl.ds(0, count * 16)]
        pltpu.make_async_copy(at, at, sem).wait()

    def await_slabs(sem, count):
        at = cpl_v.at[pl.ds(0, count * 8)]
        pltpu.make_async_copy(at, at, sem).wait()

    def zat(step):
        return chip(far_first(step))

    def block_of(step):
        return (1 - k) * 8 + step if step < 8 else k * 8 + zat(step - 8)

    def inv_load(part):
        at = rows(jnp.where(k == 0, (part + 4) % 8, part), 256)
        return pltpu.make_async_copy(inv_hbm.at[0, at], inv_v.at[at], load_sem.at[part])

    rhs_load = pltpu.make_async_copy(rhs_hbm.at[0], rhs_v, load_sem.at[8])
    cpl_load = pltpu.make_async_copy(cpl_hbm.at[0], cpl_v, load_sem.at[9])
    rinv_load = pltpu.make_async_copy(rinv_hbm, rinv_v, load_sem.at[10])
    root_load = pltpu.make_async_copy(root_hbm, root_v, load_sem.at[11])
    rhs_load.start()
    for part in range(8):
        inv_load(part).start()
    cpl_load.start()
    rinv_load.start()
    root_load.start()

    barrier = pltpu.get_barrier_semaphore()
    pl.semaphore_signal(barrier, inc=1, device_id=sib, device_id_type=MESH)
    for d in range(1, NZ):
        pl.semaphore_signal(barrier, inc=1, device_id=zdev(d), device_id_type=MESH)
    for e in range(1, NXY):
        pl.semaphore_signal(barrier, inc=1, device_id=xydev(e // 4, e % 4), device_id_type=MESH)


    count = counts[f]
    own = k * 8 + z
    rhs_load.wait()
    spot = c * 512 + lax.broadcasted_iota(jnp.int32, (512, BLK), 0)
    vec_hl[...] = jnp.concatenate(split(jnp.where(spot < count, rhs_v[...], 0.0)), axis=1)


    def z_reduce(part, rs, zs, zr):
        def copy(index, src, d):
            return rcopy(src, rs.at[index], zs, zr.at[(0, 0, 1, 2, 2, 2, 2)[index]], zdev(d))

        def send(step):
            index = {0: 0, 1: 1, 2: 2, 5: 3, 6: 4}[step]
            return copy(index, part(zat(step)), {0: 2, 1: 1, 2: -1, 5: 1, 6: -1}[step])

        def arrived(begin, end, sem):
            at = rs.at[pl.ds(begin, end - begin)]
            pltpu.make_async_copy(at, at, zr.at[sem]).wait()

        def relay():
            arrived(0, 2, 0)
            part(chip(2))[...] += rs[0] + rs[1]
            copy(5, part(chip(2)), 2).start()
            arrived(2, 3, 1)
            part(chip(-2))[...] += rs[2]
            copy(6, part(chip(-2)), -2).start()

        def total():
            arrived(3, 7, 2)
            return part(z)[...] + ((rs[3] + rs[4]) + (rs[5] + rs[6]))

        return send, relay, total

    def gather(piece, gs, gr, sr):
        def z_copy(index, d_owner, d):
            at = piece(k, chip(d_owner))
            return rcopy(at, at, gs, gr.at[index], zdev(d))

        def sib_copy(owner):
            at = piece(k, owner)
            return rcopy(at, at, gs, sr.at[owner], sib)

        def sib_arrival(owner):
            at = piece(1 - k, owner)
            return rcopy(at, at, gs, sr.at[owner], sib)

        first = [(0, 0, 2), (1, 0, -2), (2, 0, 1), (3, 0, -1)]
        second = [(4, -2, 1), (5, -2, 2), (6, 2, -1)]
        arrivals = {0: -2, 1: 2, 2: -1, 3: 1, 4: -3, 5: -4, 6: 3}

        def arrive(index):
            z_copy(index, arrivals[index], 1).wait_recv()

        def pass_on(index):
            sib_copy(chip(arrivals[index])).start()

        def start():
            for item in first:
                z_copy(*item).start()
            sib_copy(z).start()

        def relay():
            arrive(0)
            z_copy(*second[0]).start()
            z_copy(*second[1]).start()
            pass_on(0)
            arrive(1)
            z_copy(*second[2]).start()
            pass_on(1)

        def near():
            for index in (2, 3):
                arrive(index)
                pass_on(index)

        def far():
            for index in (6, 4, 5):
                arrive(index)
                pass_on(index)

        def take(begin, end, use):
            owners = [chip(d) for d in ARRIVALS[begin:end]]
            for owner in owners:
                sib_arrival(owner).wait_recv()
            return use(owners)

        return start, relay, near, far, take

    def z_reduce_direct(part, rs, zs, zr):
        def start():
            for step in range(7):
                rcopy(part(zat(step)), rs.at[step], zs, zr, zdev(far_first(step))).start()

        def total():
            pltpu.make_async_copy(rs, rs, zr).wait()
            value = part(z)[...]
            for step in range(7):
                value = value + rs[step]
            return value

        return start, total

    def gather_direct(piece, gs, gr, sr):
        def z_copy(step, owner):
            at = piece(k, owner)
            return rcopy(at, at, gs, gr.at[step], zdev(far_first(step)))

        def sib_copy(owner):
            at = piece(k, owner)
            return rcopy(at, at, gs, sr, sib)

        def start():
            for step in range(7):
                z_copy(step, z).start()
            sib_copy(z).start()

        def finish():
            for step in (5, 6, 3, 4, 1, 2, 0):
                owner = chip(-far_first(step))
                z_copy(step, owner).wait_recv()
                sib_copy(owner).start()
            await_slabs(sr, NZ)

        return start, finish


    def slab(p):
        return p % 2, rows(p // 2, 8)

    def plane_at(df, dr):
        return slab(((f + df) % 4) * 4 + (r + dr) % 4)

    here = plane_at(0, 0)

    def plane(src, recv, full, ps, pr, qr):
        def out_copy(step):
            df, dr = plane_step(step)
            return rcopy(src.at[plane_at(df, dr)], recv.at[step], ps, pr, xydev(df, dr))

        def all_copy(step):
            df, dr = plane_step(step)
            return rcopy(full.at[here], full.at[here], ps, qr, xydev(df, dr))

        def start():
            for step in range(15):
                out_copy(step).start()

        def middle(combine):
            total = src[here]
            pltpu.make_async_copy(recv, recv, pr).wait()
            for step in range(15):
                total = total + recv[step]
            full[here] = combine(total)
            for step in range(15):
                all_copy(step).start()

        def finish():
            await_slabs(qr, 15)
            return join(full[0], full[1], 1)

        return start, middle, finish


    def forward_group(group):
        steps = range(4 * group, 4 * group + 4)
        for part in ((0, 1), (2, 3), (4, 5, 6, 7), ())[group]:
            inv_load(part).wait()
        highs, lows = [], []
        for step in steps:
            at = rows(block_of(step))
            high, low = split(inv_v[at, :])
            inv_hi[at, :] = high
            inv_lo[at, :] = low
            highs.append(high)
            lows.append(low)
        value = mm(jnp.concatenate(highs + lows, axis=0), vec_hl[...])
        value = halves(value[:, :BLK] + value[:, BLK:])
        return [value[j * BLK:(j + 1) * BLK].T for j in range(4)]

    core_copy1 = rcopy(part1.at[rows(1 - k, 8)], core1, c1s, c1r, sib)

    for group in range(2):
        for j, value in enumerate(forward_group(group)):
            part1[block_of(4 * group + j)] = value
    pl.semaphore_wait(barrier, NZ + NXY - 1)
    core_copy1.start()

    src_rows = [pl.ds(0, SRC), pl.ds(SRC, SRC)]
    sum1 = [
        z_reduce(lambda owner, h=h: part1.at[k * 8 + owner, src_rows[h]], rs1.at[h], z1s, z1r.at[h])
        for h in range(2)
    ]
    for group in range(2):
        values = forward_group(group + 2)
        if not group:
            core_copy1.wait_recv()
        for j in range(4):
            owner = zat(4 * group + j)
            part1[k * 8 + owner] = values[j] + core1[owner]
        for step in ((0, 1, 2), (5, 6))[group]:
            sum1[0][0](step).start()
    for step in (0, 1, 2, 5, 6):
        sum1[1][0](step).start()

    cpl_load.wait()

    def split_cpl(i):
        at = rows(i)
        high, low = split(cpl_v[at, :])
        cpl_hi[at, :] = high
        cpl_lo[at, :] = low

    loop(16, split_cpl)

    def build_map(i):
        at = rows(i)
        spots = i * BLK + lax.broadcasted_iota(jnp.int32, (BLK, 384), 0)
        hot = (map_ref[...] - c * 768 == spots).astype(F32)
        place[at, :] = hot.astype(BF16)
        place_t[i] = hot.T.astype(BF16)

    loop(6, build_map)

    def split_rinv(i):
        at = rows(i)
        value = rinv_v[at, :]
        high, low = split(value)
        rin_hi[at, :] = high
        rin_lo[at, :] = low
        high, low = split(value.T)
        rint_hi[i] = high
        rint_lo[i] = low

    def turn_cpl(i):
        high, low = split(cpl_v[rows(i), :].T)
        cplt_hi[i] = high
        cplt_lo[i] = low

    root_load.wait()
    for i in range(6):
        turned = root_v[i * BLK:(i + 1) * BLK, :].T
        for h in range(2):
            root_t[h, i // 3, :, (i % 3) * BLK:(i % 3 + 1) * BLK] = turned[h * SRC:(h + 1) * SRC]
    live = r * 2048 + own * BLK + lax.broadcasted_iota(jnp.int32, (SRC, BLK), 1) < count

    ag1, xy2, ag3, xy4, ag5 = [], [], [], [], []
    for h in range(2):
        sum1[h][1]()
    rinv_load.wait()
    loop(6, split_rinv)
    for h in range(2):
        forward = jnp.where(live, sum1[h][2](), 0.0)
        fwd[h] = forward
        full1[h, own] = forward
        ag1.append(gather(lambda kk, zz, h=h: full1.at[h, kk * 8 + zz], g1s, g1r.at[h], s1r.at[h]))
        ag1[h][0]()

    def use_border(h):
        def use(owners):
            blocks = [side * 8 + owner for owner in owners for side in (k, 1 - k)]
            left = stack(jnp.concatenate([full1[h, block] for block in blocks], axis=1))
            high = jnp.concatenate([cpl_hi[rows(block), :] for block in blocks], axis=0)
            low = jnp.concatenate([cpl_lo[rows(block), :] for block in blocks], axis=0)
            return mm(left, high) + mm(left, low)

        return use

    for h in range(2):
        ag1[h][1]()
    for h in range(2):
        ag1[h][2]()
    for h in range(2):
        ag1[h][3]()
        acc_b[...] = ag1[h][4](0, 4, use_border(h))
        whole = halves(acc_b[...] + ag1[h][4](4, 8, use_border(h)))
        border_hl = stack(whole)
        spread = halves(mm(border_hl, jnp.concatenate([place_t[i] for i in range(6)], axis=1)))
        spread_s[h, 0] = spread[:, :384]
        spread_s[h, 1] = spread[:, 384:]
        xy2.append(plane(
            spread_s.at[h], xyr2.at[h], upd_t.at[h], p2s, p2r.at[h], q2r.at[h]
        ))
        xy2[h][0]()

    loop(8, turn_cpl)
    for h in range(2):
        xy2[h][1](lambda total, h=h: root_t.at[h][here] - total)

    def core_copy3(h):
        return rcopy(
            part3.at[h, :, rows(1 - k, 32)], core3.at[h], c3s, c3r.at[h], sib
        )

    def slab3(kk, zz):
        return zz % 2, rows(kk * 4 + zz // 2, 8)

    loop(8, lambda i: turn_cpl(i + 8))
    sum3 = []
    for h in range(2):
        upd_hl = stack(xy2[h][2]())
        value = halves(
            mm(upd_hl, jnp.concatenate([rint_hi[i] for i in range(6)], axis=1))
            + mm(upd_hl, jnp.concatenate([rint_lo[i] for i in range(6)], axis=1))
        )
        part3[h, 0] = value[:, :384]
        part3[h, 1] = value[:, 384:]
        core_copy3(h).start()
        core_copy3(h).wait_recv()
        part3[h, :, rows(k, 32)] += core3[h]
        sum3.append(z_reduce_direct(
            lambda owner, h=h: part3.at[h].at[slab3(k, owner)], rs3.at[h], z3s, z3r.at[h]
        ))
        sum3[h][0]()
    for h in range(2):
        full3.at[h][slab3(k, z)] = sum3[h][1]()
        ag3.append(gather_direct(
            lambda kk, zz, h=h: full3.at[h].at[slab3(kk, zz)], g3s, g3r.at[h], s3r.at[h]
        ))
        ag3[h][0]()

    for h in range(2):
        ag3[h][1]()
        fwd_hl = stack(join(full3[h, 0], full3[h, 1], 1))
        value = halves(mm(fwd_hl, rin_hi[...]) + mm(fwd_hl, rin_lo[...]))
        back_s[h, 0] = value[:, :384]
        back_s[h, 1] = value[:, 384:]
        xy4.append(plane(
            back_s.at[h], xyr4.at[h], back_t.at[h], p4s, p4r.at[h], q4r.at[h]
        ))
        xy4[h][0]()
    for h in range(2):
        xy4[h][1](lambda total: total)

    def core_copy5(h, group):
        src = part5.at[h, rows(2 * (1 - k) + group, 4)]
        return rcopy(src, core5.at[h, pl.ds(4 * group, 4)], c5s, c5r.at[h], sib)

    sum5 = []
    for h in range(2):
        back = xy4[h][2]()
        left = stack(halves(mm(stack(back), place[...])))

        def correction_group(group, left=left):
            blocks = [block_of(step) for step in range(4 * group, 4 * group + 4)]
            value = halves(
                mm(left, jnp.concatenate([cplt_hi[block] for block in blocks], axis=1))
                + mm(left, jnp.concatenate([cplt_lo[block] for block in blocks], axis=1))
            )
            return [value[:, j * BLK:(j + 1) * BLK] for j in range(4)]

        for group in range(2):
            for j, value in enumerate(correction_group(group)):
                part5[h, block_of(4 * group + j)] = value
            core_copy5(h, group).start()
        sum5.append(z_reduce(
            lambda owner, h=h: part5.at[h, k * 8 + owner], rs5.at[h], z5s, z5r.at[h]
        ))
        values = correction_group(2) + correction_group(3)
        for step in range(8):
            part5[h, block_of(step + 8)] = values[step]
        pltpu.make_async_copy(core5.at[h], core5.at[h], c5r.at[h]).wait()
        for step in range(8):
            owner = zat(step)
            part5[h, k * 8 + owner] += core5[h, owner]
            if step in (0, 1, 2, 5, 6):
                sum5[h][0](step).start()

    for i in range(6):
        half, at = i // 3, (i % 3) * BLK
        root_v[i * BLK:(i + 1) * BLK, :] = join(back_t[0, half, :, at:at + BLK], back_t[1, half, :, at:at + BLK], 0).T
    root_store = pltpu.make_async_copy(root_v, root_out, out_sem.at[0])
    root_store.start()

    for h in range(2):
        sum5[h][1]()
    for h in range(2):
        full5[h, own] = jnp.where(live, fwd[h] - sum5[h][2](), 0.0)
        ag5.append(gather(lambda kk, zz, h=h: full5.at[h, kk * 8 + zz], g5s, g5r.at[h], s5r.at[h]))
        ag5[h][0]()

    def yslab(d):
        return rows((r + d) % 4, 16)

    def ydev(d):
        return (f, (r + d) % 4, c)

    def y_copy(h, d):
        return rcopy(ypart.at[h, yslab(d)], yrs.at[h, d - 1], y6s, y6r.at[h], ydev(d))

    def w_copy(h, d):
        return rcopy(yfull.at[h, yslab(0)], yfull.at[h, yslab(0)], y6s, w6r.at[h], ydev(d))

    def use_back(h):
        def use(owners):
            blocks = [side * 8 + owner for owner in owners for side in (k, 1 - k)]
            left = stack(jnp.concatenate([full5[h, block] for block in blocks], axis=1))
            high = jnp.concatenate([inv_hi[rows(block), :] for block in blocks], axis=0)
            low = jnp.concatenate([inv_lo[rows(block), :] for block in blocks], axis=0)
            return mm(left, high) + mm(left, low)

        return use

    for h in range(2):
        ag5[h][1]()
    for h in range(2):
        ag5[h][2]()
    for h in range(2):
        ag5[h][3]()
        acc_c[...] = ag5[h][4](0, 4, use_back(h))
        whole = halves(acc_c[...] + ag5[h][4](4, 8, use_back(h)))
        ypart[h] = whole
        for d in (2, 1, 3):
            y_copy(h, d).start()
    for h in range(2):
        total = ypart[h, yslab(0)]
        pltpu.make_async_copy(yrs.at[h], yrs.at[h], y6r.at[h]).wait()
        for d in (1, 3, 2):
            total = total + yrs[h, d - 1]
        yfull[h, yslab(0)] = total
        for d in (2, 1, 3):
            w_copy(h, d).start()
    for h in range(2):
        await_blocks(w6r.at[h], 3)
    for i in range(4):
        at = c * 512 + i * BLK + lax.broadcasted_iota(jnp.int32, (BLK, BLK), 0)
        value = join(yfull[0, :, i * BLK:(i + 1) * BLK], yfull[1, :, i * BLK:(i + 1) * BLK], 0).T
        rhs_v[i * BLK:(i + 1) * BLK, :] = jnp.where(at < count, value, 0.0)
    child_store = pltpu.make_async_copy(rhs_v, child_out.at[0], out_sem.at[1])
    child_store.start()
    await_blocks(c1s, 8 * 2)
    await_blocks(z1s, 2 * 7)
    await_blocks(g1s, 2 * 15)
    await_slabs(p2s, 2 * 30)
    await_slabs(c3s, 2 * 8)
    await_slabs(z3s, 2 * 7)
    await_slabs(g3s, 2 * 15)
    await_slabs(p4s, 2 * 30)
    await_blocks(c5s, 2 * 8)
    await_blocks(z5s, 2 * 7)
    await_blocks(g5s, 2 * 15)
    await_blocks(y6s, 2 * 6)
    root_store.wait()
    child_store.wait()


def hand_over(child, root, child_out, root_out, child_v, root_v, sems):
    loads = [
        pltpu.make_async_copy(child, child_v, sems.at[0]),
        pltpu.make_async_copy(root, root_v, sems.at[1]),
    ]
    stores = [
        pltpu.make_async_copy(child_v, child_out, sems.at[2]),
        pltpu.make_async_copy(root_v, root_out, sems.at[3]),
    ]
    for load in loads:
        load.start()
    for load, store in zip(loads, stores):
        load.wait()
        store.start()
    for store in stores:
        store.wait()


def per_device(child_rhs, root_rhs, child_inv, coupling, root_inv, pivot_counts, border_map):
    def v(*shape, dtype=F32):
        return pltpu.VMEM(shape, dtype)

    dma = pltpu.SemaphoreType.DMA
    scratch = [
        v(512, 128), v(768, 128), v(2048, 512), v(2048, 384), v(768, 768),
        v(2048, 512, dtype=BF16), v(2048, 512, dtype=BF16), v(2048, 384, dtype=BF16), v(2048, 384, dtype=BF16),
        v(768, 768, dtype=BF16), v(768, 768, dtype=BF16),
        v(512, 256, dtype=BF16), v(768, 384, dtype=BF16), v(6, 384, 128, dtype=BF16),
        v(16, 384, 128, dtype=BF16), v(16, 384, 128, dtype=BF16),
        v(6, 768, 128, dtype=BF16), v(6, 768, 128, dtype=BF16), v(2, 2, 64, 384), v(2, 64, 128),
        v(16, 128, 128), v(8, 128, 128), v(2, 7, 64, 128), v(2, 16, 64, 128),
        v(2, 16, 64, 128), v(2, 8, 64, 128), v(2, 7, 64, 128), v(2, 16, 64, 128),
        v(2, 2, 64, 384), v(2, 15, 8, 384), v(2, 2, 64, 384),
        v(2, 2, 64, 384), v(2, 2, 32, 384), v(2, 7, 8, 384), v(2, 2, 64, 384),
        v(2, 2, 64, 384), v(2, 15, 8, 384), v(2, 2, 64, 384),
        v(128, 384), v(128, 512),
        v(2, 64, 512), v(2, 3, 16, 512), v(2, 64, 512),
        dma((12,)), dma((2,)),
    ]
    scratch += [dma] * 12
    scratch += [dma, dma((2, 3)), dma((2, 7)), dma((2, 8))]
    scratch += [dma((2,)), dma((2,)), dma((2, 7)), dma((2,))]
    scratch += [dma((2,)), dma((2, 3)), dma((2, 7)), dma((2, 8))]
    scratch += [dma((2,))] * 6
    hbm = pl.BlockSpec(memory_space=pl.ANY)
    results = tuple(
        pl.pallas_call(
            kernel,
            out_shape=(
                jax.ShapeDtypeStruct((1, 512, 128), F32),
                jax.ShapeDtypeStruct((768, 128), F32),
            ),
            in_specs=[hbm] * 5
            + [pl.BlockSpec(memory_space=pltpu.SMEM), pl.BlockSpec(memory_space=pltpu.VMEM)],
            out_specs=(hbm, hbm),
            scratch_shapes=scratch,
            compiler_params=pltpu.CompilerParams(
                collective_id=0, has_side_effects=True, vmem_limit_bytes=56 << 20
            ),
            cost_estimate=pl.CostEstimate(flops=5 * 10**9, bytes_accessed=11 * 10**6, transcendentals=0),
        )(child_rhs, root_rhs, child_inv, coupling, root_inv, pivot_counts, border_map)
    )
    return tuple(
        pl.pallas_call(
            hand_over,
            out_shape=tuple(jax.ShapeDtypeStruct(a.shape, a.dtype) for a in results),
            in_specs=[hbm] * 2,
            out_specs=(hbm, hbm),
            scratch_shapes=[v(1, 512, 128), v(768, 128), dma((4,))],
            compiler_params=pltpu.CompilerParams(vmem_limit_bytes=56 << 20),
        )(*results)
    )


def solution(mesh):
    in_specs = (
        P("front", "col", None),
        P("col", None),
        P("front", "row", "col"),
        P("front", "row", "col"),
        P(("front", "row"), "col"),
        P(),
        P("front", "col"),
    )
    out_specs = (P("front", "col", None), P("col", None))
    return jax.shard_map(
        per_device, mesh=mesh, in_specs=in_specs, out_specs=out_specs, check_vma=False
    )
```

```python
import jax
import jax.numpy as jnp
from jax import lax
from jax.experimental import pallas as pl
from jax.experimental.pallas import tpu as pltpu
from jax.sharding import PartitionSpec as P

MESH = pl.DeviceIdType.MESH
F32 = jnp.float32
BF16 = jnp.bfloat16
NZ = 8
NXY = 16
BLK = 128
SRC = 64
PLANE = (
    (2, 2), (2, 1), (2, 3), (1, 2), (3, 2), (2, 0), (0, 2), (1, 1),
    (3, 3), (1, 3), (3, 1), (0, 1), (0, 3), (1, 0), (3, 0),
)
ARRIVALS = (0, -2, 2, -1, 1, 3, -3, -4)


def split(value):
    high = value.astype(BF16)
    low = (value - high.astype(F32)).astype(BF16)
    return high, low


def stack(value):
    return jnp.concatenate(split(value), axis=0)


def mm(left, right):
    return jnp.dot(left, right, preferred_element_type=F32)


def mm_split(left, high, low):
    return mm(jnp.concatenate([left, left], axis=1), jnp.concatenate([high, low], axis=0))


def halves(value):
    rows = value.shape[0] // 2
    return value[:rows] + value[rows:]


def join(left, right, axis):
    return jnp.concatenate([left, right], axis=axis)


def far_first(step):
    return 4 + (1 - 2 * (step % 2)) * ((step + 1) // 2)


def loop(n, body):
    def step(i, carry):
        body(i)
        return carry

    lax.fori_loop(0, n, step, 0)


def rows(block, size=BLK):
    return pl.ds(pl.multiple_of(block * size, size), size)


def kernel(
    rhs_hbm, root_hbm, inv_hbm, cpl_hbm, rinv_hbm, counts_hbm, map_hbm,
    child_out, root_out,
    rhs_v, root_v, inv_v, cpl_v, rinv_v,
    inv_hi, inv_lo, cpl_hi, cpl_lo, rin_hi, rin_lo,
    vec_hl, place, place_t, cplt_hi, cplt_lo, rint_hi, rint_lo, root_t, fwd,
    part1, core1, rs1, full1,
    part5, core5, rs5, full5,
    spread_s, xyr2, upd_t,
    part3, core3, rs3, full3,
    back_s, xyr4, back_t,
    acc_b, acc_c,
    ypart, yrs, yfull,
    counts, map_ref, load_sem, out_sem,
    c1s, z1s, g1s, p2s, c3s, z3s, g3s, p4s, c5s, z5s, g5s, y6s,
    c1r, z1r, g1r, s1r, c3r, z3r, g3r, s3r, c5r, z5r, g5r, s5r,
    p2r, q2r, p4r, q4r, y6r, w6r,
):
    f = lax.axis_index("front")
    r = lax.axis_index("row")
    c = lax.axis_index("col")
    z = c // 2
    k = c % 2
    sib = (f, r, z * 2 + (1 - k))

    way = 1 - 2 * k

    def chip(d):
        return (z + way * d + 2 * NZ) % NZ

    def zdev(d):
        return (f, r, chip(d) * 2 + k)

    def xydev(df, dr):
        return ((f + df) % 4, (r + dr) % 4, c)

    def rcopy(src, dst, ss, rs, dev):
        return pltpu.make_async_remote_copy(
            src_ref=src, dst_ref=dst, send_sem=ss, recv_sem=rs, device_id=dev, device_id_type=MESH
        )

    def await_blocks(sem, count):
        at = inv_v.at[pl.ds(0, count * 16)]
        pltpu.make_async_copy(at, at, sem).wait()

    def await_slabs(sem, count):
        at = cpl_v.at[pl.ds(0, count * 8)]
        pltpu.make_async_copy(at, at, sem).wait()

    def zat(step):
        return chip(far_first(step))

    def block_of(step):
        return (1 - k) * 8 + step if step < 8 else k * 8 + zat(step - 8)

    def inv_load(part):
        at = rows(jnp.where(k == 0, (part + 4) % 8, part), 256)
        return pltpu.make_async_copy(inv_hbm.at[0, at], inv_v.at[at], load_sem.at[part])

    rhs_load = pltpu.make_async_copy(rhs_hbm.at[0], rhs_v, load_sem.at[8])
    cpl_load = pltpu.make_async_copy(cpl_hbm.at[0], cpl_v, load_sem.at[9])
    rinv_load = pltpu.make_async_copy(rinv_hbm, rinv_v, load_sem.at[10])
    root_load = pltpu.make_async_copy(root_hbm, root_v, load_sem.at[11])
    counts_load = pltpu.make_async_copy(counts_hbm, counts, load_sem.at[12])
    map_load = pltpu.make_async_copy(map_hbm, map_ref, load_sem.at[13])
    counts_load.start()
    rhs_load.start()
    for part in range(8):
        inv_load(part).start()
    map_load.start()
    cpl_load.start()
    rinv_load.start()
    root_load.start()

    barrier = pltpu.get_barrier_semaphore()
    pl.semaphore_signal(barrier, inc=1, device_id=sib, device_id_type=MESH)
    for d in range(1, NZ):
        pl.semaphore_signal(barrier, inc=1, device_id=zdev(d), device_id_type=MESH)
    for e in range(1, NXY):
        pl.semaphore_signal(barrier, inc=1, device_id=xydev(e // 4, e % 4), device_id_type=MESH)


    counts_load.wait()
    count = counts[f]
    own = k * 8 + z
    rhs_load.wait()
    spot = c * 512 + lax.broadcasted_iota(jnp.int32, (512, BLK), 0)
    vector = jnp.concatenate(split(jnp.where(spot < count, rhs_v[...], 0.0)), axis=1)
    vec_hl[:512, :] = vector
    vec_hl[512:, :] = vector


    def z_reduce(part, rs, zs, zr):
        def copy(index, src, d):
            return rcopy(src, rs.at[index], zs, zr.at[(0, 0, 1, 2, 2, 2, 2)[index]], zdev(d))

        def send(step):
            index = {0: 0, 1: 1, 2: 2, 5: 3, 6: 4}[step]
            return copy(index, part(zat(step)), {0: 2, 1: 1, 2: -1, 5: 1, 6: -1}[step])

        def arrived(begin, end, sem):
            at = rs.at[pl.ds(begin, end - begin)]
            pltpu.make_async_copy(at, at, zr.at[sem]).wait()

        def relay():
            arrived(0, 2, 0)
            part(chip(2))[...] += rs[0] + rs[1]
            copy(5, part(chip(2)), 2).start()
            arrived(2, 3, 1)
            part(chip(-2))[...] += rs[2]
            copy(6, part(chip(-2)), -2).start()

        def total():
            arrived(3, 7, 2)
            return part(z)[...] + ((rs[3] + rs[4]) + (rs[5] + rs[6]))

        return send, relay, total

    def gather(piece, gs, gr, sr):
        def z_copy(index, d_owner, d):
            at = piece(k, chip(d_owner))
            return rcopy(at, at, gs, gr.at[index], zdev(d))

        def sib_copy(owner):
            at = piece(k, owner)
            return rcopy(at, at, gs, sr.at[owner], sib)

        def sib_arrival(owner):
            at = piece(1 - k, owner)
            return rcopy(at, at, gs, sr.at[owner], sib)

        first = [(0, 0, 2), (1, 0, -2), (2, 0, 1), (3, 0, -1)]
        second = [(4, -2, 1), (5, -2, 2), (6, 2, -1)]
        arrivals = {0: -2, 1: 2, 2: -1, 3: 1, 4: -3, 5: -4, 6: 3}

        def arrive(index):
            z_copy(index, arrivals[index], 1).wait_recv()

        def pass_on(index):
            sib_copy(chip(arrivals[index])).start()

        def start():
            for item in first:
                z_copy(*item).start()
            sib_copy(z).start()

        def relay():
            arrive(0)
            z_copy(*second[0]).start()
            z_copy(*second[1]).start()
            pass_on(0)
            arrive(1)
            z_copy(*second[2]).start()
            pass_on(1)

        def near():
            for index in (2, 3):
                arrive(index)
                pass_on(index)

        def far():
            for index in (6, 4, 5):
                arrive(index)
                pass_on(index)

        def take(begin, end, use):
            owners = [chip(d) for d in ARRIVALS[begin:end]]
            for owner in owners:
                sib_arrival(owner).wait_recv()
            return use(owners)

        return start, relay, near, far, take

    def z_reduce_direct(part, rs, zs, zr):
        def start():
            for step in range(7):
                rcopy(part(zat(step)), rs.at[step], zs, zr, zdev(far_first(step))).start()

        def total():
            pltpu.make_async_copy(rs, rs, zr).wait()
            value = part(z)[...]
            for step in range(7):
                value = value + rs[step]
            return value

        return start, total

    def gather_direct(piece, gs, gr, sr):
        def z_copy(step, owner):
            at = piece(k, owner)
            return rcopy(at, at, gs, gr.at[step], zdev(far_first(step)))

        def sib_copy(owner):
            at = piece(k, owner)
            return rcopy(at, at, gs, sr, sib)

        def start():
            for step in range(7):
                z_copy(step, z).start()
            sib_copy(z).start()

        def finish():
            for step in (5, 6, 3, 4, 1, 2, 0):
                owner = chip(-far_first(step))
                z_copy(step, owner).wait_recv()
                sib_copy(owner).start()
            await_slabs(sr, NZ)

        return start, finish


    def slab(p):
        return p % 2, rows(p // 2, 8)

    def plane_at(df, dr):
        return slab(((f + df) % 4) * 4 + (r + dr) % 4)

    here = plane_at(0, 0)

    def plane(src, recv, full, ps, pr, qr):
        def out_copy(step):
            df, dr = PLANE[step]
            return rcopy(src.at[plane_at(df, dr)], recv.at[step], ps, pr, xydev(df, dr))

        def all_copy(step):
            df, dr = PLANE[step]
            return rcopy(full.at[here], full.at[here], ps, qr, xydev(df, dr))

        def start():
            for step in range(15):
                out_copy(step).start()

        def middle(combine):
            total = src[here]
            pltpu.make_async_copy(recv, recv, pr).wait()
            for step in range(15):
                total = total + recv[step]
            full[here] = combine(total)
            for step in range(15):
                all_copy(step).start()

        def finish():
            await_slabs(qr, 15)
            return join(full[0], full[1], 1)

        return start, middle, finish


    def forward_group(group):
        steps = range(4 * group, 4 * group + 4)
        for part in ((0, 1), (2, 3), (4, 5, 6, 7), ())[group]:
            inv_load(part).wait()
        highs, lows = [], []
        for step in steps:
            at = rows(block_of(step))
            high, low = split(inv_v[at, :])
            highs.append(high)
            lows.append(low)
        values = []
        for high, low in zip(highs, lows):
            value = mm(join(high, low, 1), vec_hl[...])
            values.append((value[:, :BLK] + value[:, BLK:]).T)
        return values

    core_copy1 = rcopy(part1.at[rows(1 - k, 8)], core1, c1s, c1r, sib)

    for group in range(2):
        for j, value in enumerate(forward_group(group)):
            part1[block_of(4 * group + j)] = value
    pl.semaphore_wait(barrier, NZ + NXY - 1)
    core_copy1.start()

    src_rows = [pl.ds(0, SRC), pl.ds(SRC, SRC)]
    sum1 = [
        z_reduce(lambda owner, h=h: part1.at[k * 8 + owner, src_rows[h]], rs1.at[h], z1s, z1r.at[h])
        for h in range(2)
    ]
    for group in range(2):
        values = forward_group(group + 2)
        if not group:
            core_copy1.wait_recv()
        for j in range(4):
            owner = zat(4 * group + j)
            part1[k * 8 + owner] = values[j] + core1[owner]
        for step in ((0, 1, 2), (5, 6))[group]:
            sum1[0][0](step).start()
    for step in (0, 1, 2, 5, 6):
        sum1[1][0](step).start()

    cpl_load.wait()

    def split_cpl(i):
        at = rows(i)
        high, low = split(cpl_v[at, :])
        cpl_hi[at, :] = high
        cpl_lo[at, :] = low

    loop(16, split_cpl)

    def build_map(i):
        at = rows(i)
        spots = i * BLK + lax.broadcasted_iota(jnp.int32, (BLK, 384), 0)
        hot = (map_ref[...] - c * 768 == spots).astype(F32)
        place[at, :] = hot.astype(BF16)
        place_t[i] = hot.T.astype(BF16)

    map_load.wait()
    loop(6, build_map)

    def split_rinv(i):
        at = rows(i)
        value = rinv_v[at, :]
        high, low = split(value)
        rin_hi[at, :] = high
        rin_lo[at, :] = low
        high, low = split(value.T)
        rint_hi[i] = high
        rint_lo[i] = low

    def split_inv(i):
        at = rows(i)
        high, low = split(inv_v[at, :])
        inv_hi[at, :] = high
        inv_lo[at, :] = low

    def turn_cpl(i):
        high, low = split(cpl_v[rows(i), :].T)
        cplt_hi[i] = high
        cplt_lo[i] = low

    root_load.wait()
    for i in range(6):
        turned = root_v[i * BLK:(i + 1) * BLK, :].T
        for h in range(2):
            root_t[h, i // 3, :, (i % 3) * BLK:(i % 3 + 1) * BLK] = turned[h * SRC:(h + 1) * SRC]
    live = r * 2048 + own * BLK + lax.broadcasted_iota(jnp.int32, (SRC, BLK), 1) < count

    ag1, xy2, ag3, xy4, ag5 = [], [], [], [], []
    for h in range(2):
        sum1[h][1]()
    rinv_load.wait()
    loop(6, split_rinv)
    for h in range(2):
        forward = jnp.where(live, sum1[h][2](), 0.0)
        fwd[h] = forward
        full1[h, own] = forward
        ag1.append(gather(lambda kk, zz, h=h: full1.at[h, kk * 8 + zz], g1s, g1r.at[h], s1r.at[h]))
        ag1[h][0]()

    def use_border(h):
        def use(owners):
            blocks = [side * 8 + owner for owner in owners for side in (k, 1 - k)]
            left = stack(jnp.concatenate([full1[h, block] for block in blocks], axis=1))
            high = jnp.concatenate([cpl_hi[rows(block), :] for block in blocks], axis=0)
            low = jnp.concatenate([cpl_lo[rows(block), :] for block in blocks], axis=0)
            return mm_split(left, high, low)

        return use

    for h in range(2):
        ag1[h][1]()
    for h in range(2):
        ag1[h][2]()
    for h in range(2):
        ag1[h][3]()
        acc_b[...] = ag1[h][4](0, 4, use_border(h))
        whole = halves(acc_b[...] + ag1[h][4](4, 8, use_border(h)))
        border_hl = stack(whole)
        spread = halves(mm(border_hl, jnp.concatenate([place_t[i] for i in range(6)], axis=1)))
        spread_s[h, 0] = spread[:, :384]
        spread_s[h, 1] = spread[:, 384:]
        xy2.append(plane(
            spread_s.at[h], xyr2.at[h], upd_t.at[h], p2s, p2r.at[h], q2r.at[h]
        ))
        xy2[h][0]()

    loop(8, turn_cpl)
    for h in range(2):
        xy2[h][1](lambda total, h=h: root_t.at[h][here] - total)

    def core_copy3(h):
        return rcopy(
            part3.at[h, 1 - k], core3.at[h], c3s, c3r.at[h], sib
        )

    def slab3(kk, zz):
        return kk, rows(zz, 8)

    loop(8, lambda i: turn_cpl(i + 8))
    sum3 = []
    for h in range(2):
        upd_hl = stack(xy2[h][2]())
        for side in (1 - k, k):
            blocks = [side * 3 + i for i in range(3)]
            part3[h, side] = halves(
                mm_split(
                    upd_hl,
                    jnp.concatenate([rint_hi[block] for block in blocks], axis=1),
                    jnp.concatenate([rint_lo[block] for block in blocks], axis=1),
                )
            )
            if side is not k:
                core_copy3(h).start()
        core_copy3(h).wait_recv()
        part3[h, k] += core3[h]
        sum3.append(z_reduce_direct(
            lambda owner, h=h: part3.at[h].at[slab3(k, owner)], rs3.at[h], z3s, z3r.at[h]
        ))
        sum3[h][0]()
    loop(16, split_inv)
    for h in range(2):
        full3.at[h][slab3(k, z)] = sum3[h][1]()
        ag3.append(gather_direct(
            lambda kk, zz, h=h: full3.at[h].at[slab3(kk, zz)], g3s, g3r.at[h], s3r.at[h]
        ))
        ag3[h][0]()

    for h in range(2):
        ag3[h][1]()
        fwd_hl = stack(join(full3[h, 0], full3[h, 1], 1))
        value = halves(mm_split(fwd_hl, rin_hi[...], rin_lo[...]))
        back_s[h, 0] = value[:, :384]
        back_s[h, 1] = value[:, 384:]
        xy4.append(plane(
            back_s.at[h], xyr4.at[h], back_t.at[h], p4s, p4r.at[h], q4r.at[h]
        ))
        xy4[h][0]()
    for h in range(2):
        xy4[h][1](lambda total: total)

    def core_copy5(h, group):
        src = part5.at[h, rows(2 * (1 - k) + group, 4)]
        return rcopy(src, core5.at[h, pl.ds(4 * group, 4)], c5s, c5r.at[h], sib)

    sum5 = []
    for h in range(2):
        back = xy4[h][2]()
        left = stack(halves(mm(stack(back), place[...])))

        def correction_group(group, left=left):
            blocks = [block_of(step) for step in range(4 * group, 4 * group + 4)]
            value = halves(
                mm_split(
                    left,
                    jnp.concatenate([cplt_hi[block] for block in blocks], axis=1),
                    jnp.concatenate([cplt_lo[block] for block in blocks], axis=1),
                )
            )
            return [value[:, j * BLK:(j + 1) * BLK] for j in range(4)]

        for group in range(2):
            for j, value in enumerate(correction_group(group)):
                part5[h, block_of(4 * group + j)] = value
            core_copy5(h, group).start()
        sum5.append(z_reduce(
            lambda owner, h=h: part5.at[h, k * 8 + owner], rs5.at[h], z5s, z5r.at[h]
        ))
        values = correction_group(2) + correction_group(3)
        for step in range(8):
            part5[h, block_of(step + 8)] = values[step]
        pltpu.make_async_copy(core5.at[h], core5.at[h], c5r.at[h]).wait()
        for step in range(8):
            owner = zat(step)
            part5[h, k * 8 + owner] += core5[h, owner]
            if step in (0, 1, 2, 5, 6):
                sum5[h][0](step).start()

    for i in range(6):
        half, at = i // 3, (i % 3) * BLK
        root_v[i * BLK:(i + 1) * BLK, :] = join(back_t[0, half, :, at:at + BLK], back_t[1, half, :, at:at + BLK], 0).T
    root_store = pltpu.make_async_copy(root_v, root_out, out_sem.at[0])
    root_store.start()

    for h in range(2):
        sum5[h][1]()
    for h in range(2):
        full5[h, own] = jnp.where(live, fwd[h] - sum5[h][2](), 0.0)
        ag5.append(gather(lambda kk, zz, h=h: full5.at[h, kk * 8 + zz], g5s, g5r.at[h], s5r.at[h]))
        ag5[h][0]()

    def yslab(d):
        return rows((r + d) % 4, 16)

    def ydev(d):
        return (f, (r + d) % 4, c)

    def y_copy(h, d):
        return rcopy(ypart.at[h, yslab(d)], yrs.at[h, d - 1], y6s, y6r.at[h], ydev(d))

    def w_copy(h, d):
        return rcopy(yfull.at[h, yslab(0)], yfull.at[h, yslab(0)], y6s, w6r.at[h], ydev(d))

    def use_back(h):
        def use(owners):
            blocks = [side * 8 + owner for owner in owners for side in (k, 1 - k)]
            left = stack(jnp.concatenate([full5[h, block] for block in blocks], axis=1))
            high = jnp.concatenate([inv_hi[rows(block), :] for block in blocks], axis=0)
            low = jnp.concatenate([inv_lo[rows(block), :] for block in blocks], axis=0)
            return mm_split(left, high, low)

        return use

    for h in range(2):
        ag5[h][1]()
    for h in range(2):
        ag5[h][2]()
    for h in range(2):
        ag5[h][3]()
        acc_c[...] = ag5[h][4](0, 4, use_back(h))
        whole = halves(acc_c[...] + ag5[h][4](4, 8, use_back(h)))
        ypart[h] = whole
        for d in (2, 1, 3):
            y_copy(h, d).start()
    for h in range(2):
        total = ypart[h, yslab(0)]
        pltpu.make_async_copy(yrs.at[h], yrs.at[h], y6r.at[h]).wait()
        for d in (1, 3, 2):
            total = total + yrs[h, d - 1]
        yfull[h, yslab(0)] = total
        for d in (2, 1, 3):
            w_copy(h, d).start()
    for h in range(2):
        await_blocks(w6r.at[h], 3)
    for i in range(4):
        at = c * 512 + i * BLK + lax.broadcasted_iota(jnp.int32, (BLK, BLK), 0)
        value = join(yfull[0, :, i * BLK:(i + 1) * BLK], yfull[1, :, i * BLK:(i + 1) * BLK], 0).T
        rhs_v[i * BLK:(i + 1) * BLK, :] = jnp.where(at < count, value, 0.0)
    child_store = pltpu.make_async_copy(rhs_v, child_out.at[0], out_sem.at[1])
    child_store.start()
    await_blocks(c1s, 8 * 2)
    await_blocks(z1s, 2 * 7)
    await_blocks(g1s, 2 * 15)
    await_slabs(p2s, 2 * 30)
    await_slabs(c3s, 2 * 8)
    await_slabs(z3s, 2 * 7)
    await_slabs(g3s, 2 * 15)
    await_slabs(p4s, 2 * 30)
    await_blocks(c5s, 2 * 8)
    await_blocks(z5s, 2 * 7)
    await_blocks(g5s, 2 * 15)
    await_blocks(y6s, 2 * 6)
    root_store.wait()
    child_store.wait()


def hand_over(child, root, child_out, root_out, child_v, root_v, sems):
    loads = [
        pltpu.make_async_copy(child, child_v, sems.at[0]),
        pltpu.make_async_copy(root, root_v, sems.at[1]),
    ]
    stores = [
        pltpu.make_async_copy(child_v, child_out, sems.at[2]),
        pltpu.make_async_copy(root_v, root_out, sems.at[3]),
    ]
    for load in loads:
        load.start()
    for load, store in zip(loads, stores):
        load.wait()
        store.start()
    for store in stores:
        store.wait()


def per_device(child_rhs, root_rhs, child_inv, coupling, root_inv, pivot_counts, border_map):
    def v(*shape, dtype=F32):
        return pltpu.VMEM(shape, dtype)

    dma = pltpu.SemaphoreType.DMA
    scratch = [
        v(512, 128), v(768, 128), v(2048, 512), v(2048, 384), v(768, 768),
        v(2048, 512, dtype=BF16), v(2048, 512, dtype=BF16), v(2048, 384, dtype=BF16), v(2048, 384, dtype=BF16),
        v(768, 768, dtype=BF16), v(768, 768, dtype=BF16),
        v(1024, 256, dtype=BF16), v(768, 384, dtype=BF16), v(6, 384, 128, dtype=BF16),
        v(16, 384, 128, dtype=BF16), v(16, 384, 128, dtype=BF16),
        v(6, 768, 128, dtype=BF16), v(6, 768, 128, dtype=BF16), v(2, 2, 64, 384), v(2, 64, 128),
        v(16, 128, 128), v(8, 128, 128), v(2, 7, 64, 128), v(2, 16, 64, 128),
        v(2, 16, 64, 128), v(2, 8, 64, 128), v(2, 7, 64, 128), v(2, 16, 64, 128),
        v(2, 2, 64, 384), v(2, 15, 8, 384), v(2, 2, 64, 384),
        v(2, 2, 64, 384), v(2, 64, 384), v(2, 7, 8, 384), v(2, 2, 64, 384),
        v(2, 2, 64, 384), v(2, 15, 8, 384), v(2, 2, 64, 384),
        v(128, 384), v(128, 512),
        v(2, 64, 512), v(2, 3, 16, 512), v(2, 64, 512),
        pltpu.SMEM((4,), jnp.int32), pltpu.VMEM((1, 384), jnp.int32), dma((14,)), dma((2,)),
    ]
    scratch += [dma] * 12
    scratch += [dma, dma((2, 3)), dma((2, 7)), dma((2, 8))]
    scratch += [dma((2,)), dma((2,)), dma((2, 7)), dma((2,))]
    scratch += [dma((2,)), dma((2, 3)), dma((2, 7)), dma((2, 8))]
    scratch += [dma((2,))] * 6
    hbm = pl.BlockSpec(memory_space=pl.ANY)
    results = tuple(
        pl.pallas_call(
            kernel,
            out_shape=(
                jax.ShapeDtypeStruct((1, 512, 128), F32),
                jax.ShapeDtypeStruct((768, 128), F32),
            ),
            in_specs=[hbm] * 7,
            out_specs=(hbm, hbm),
            scratch_shapes=scratch,
            compiler_params=pltpu.CompilerParams(
                collective_id=0, has_side_effects=True, vmem_limit_bytes=56 << 20
            ),
            cost_estimate=pl.CostEstimate(flops=5 * 10**9, bytes_accessed=11 * 10**6, transcendentals=0),
        )(child_rhs, root_rhs, child_inv, coupling, root_inv, pivot_counts, border_map)
    )
    return tuple(
        pl.pallas_call(
            hand_over,
            out_shape=tuple(jax.ShapeDtypeStruct(a.shape, a.dtype) for a in results),
            in_specs=[hbm] * 2,
            out_specs=(hbm, hbm),
            scratch_shapes=[v(1, 512, 128), v(768, 128), dma((4,))],
            compiler_params=pltpu.CompilerParams(vmem_limit_bytes=56 << 20),
        )(*results)
    )


def solution(mesh):
    in_specs = (
        P("front", "col", None),
        P("col", None),
        P("front", "row", "col"),
        P("front", "row", "col"),
        P(("front", "row"), "col"),
        P(),
        P("front", "col"),
    )
    out_specs = (P("front", "col", None), P("col", None))
    return jax.shard_map(
        per_device, mesh=mesh, in_specs=in_specs, out_specs=out_specs, check_vma=False
    )
```

```python
import jax
import jax.numpy as jnp
from jax import lax
from jax.experimental import pallas as pl
from jax.experimental.pallas import tpu as pltpu
from jax.sharding import PartitionSpec as P

MESH = pl.DeviceIdType.MESH
F32 = jnp.float32
BF16 = jnp.bfloat16
NZ = 8
NXY = 16
BLK = 128
SRC = 64
QSRC = 32
PLANE = (
    (2, 2), (2, 1), (2, 3), (1, 2), (3, 2), (2, 0), (0, 2), (1, 1),
    (3, 3), (1, 3), (3, 1), (0, 1), (0, 3), (1, 0), (3, 0),
)
ARRIVALS = (0, -2, 2, -1, 1, 3, -3, -4)


def split(value):
    high = value.astype(BF16)
    low = (value - high.astype(F32)).astype(BF16)
    return high, low


def stack(value):
    return jnp.concatenate(split(value), axis=0)


def mm(left, right):
    return jnp.dot(left, right, preferred_element_type=F32)


def mm_split(left, high, low):
    return mm(jnp.concatenate([left, left], axis=1), jnp.concatenate([high, low], axis=0))


def halves(value):
    rows = value.shape[0] // 2
    return value[:rows] + value[rows:]


def join(left, right, axis):
    return jnp.concatenate([left, right], axis=axis)


def far_first(step):
    return 4 + (1 - 2 * (step % 2)) * ((step + 1) // 2)


def loop(n, body):
    def step(i, carry):
        body(i)
        return carry

    lax.fori_loop(0, n, step, 0)


def rows(block, size=BLK):
    return pl.ds(pl.multiple_of(block * size, size), size)


def kernel(
    rhs_hbm, root_hbm, inv_hbm, cpl_hbm, rinv_hbm, counts_hbm, map_hbm,
    child_out, root_out,
    rhs_v, root_v, inv_v, cpl_v, rinv_v,
    inv_hi, inv_lo, cpl_hi, cpl_lo, rin_hi, rin_lo,
    vec_hl, place, place_t, cplt_hi, cplt_lo, rint_hi, rint_lo, root_t, fwd,
    part1, core1, rs1, full1,
    part5, core5, rs5, full5,
    spread_s, xyr2, upd_t,
    part3, core3, rs3, full3,
    back_s, xyr4, back_t,
    acc_b, acc_c,
    ypart, yrs, yfull,
    counts, map_ref, load_sem, out_sem,
    c1s, z1s, g1s, p2s, c3s, z3s, g3s, p4s, c5s, z5s, g5s, y6s,
    c1r, z1r, g1r, s1r, c3r, z3r, g3r, s3r, c5r, z5r, g5r, s5r,
    p2r, q2r, p4r, q4r, y6r, w6r,
):
    f = lax.axis_index("front")
    r = lax.axis_index("row")
    c = lax.axis_index("col")
    z = c // 2
    k = c % 2
    sib = (f, r, z * 2 + (1 - k))

    way = 1 - 2 * k

    def chip(d):
        return (z + way * d + 2 * NZ) % NZ

    def zdev(d):
        return (f, r, chip(d) * 2 + k)

    def xydev(df, dr):
        return ((f + df) % 4, (r + dr) % 4, c)

    def rcopy(src, dst, ss, rs, dev):
        return pltpu.make_async_remote_copy(
            src_ref=src, dst_ref=dst, send_sem=ss, recv_sem=rs, device_id=dev, device_id_type=MESH
        )

    def await_blocks(sem, count):
        at = inv_v.at[pl.ds(0, count * 16)]
        pltpu.make_async_copy(at, at, sem).wait()

    def await_slabs(sem, count):
        at = cpl_v.at[pl.ds(0, count * 8)]
        pltpu.make_async_copy(at, at, sem).wait()

    def zat(step):
        return chip(far_first(step))

    def block_of(step):
        return (1 - k) * 8 + step if step < 8 else k * 8 + zat(step - 8)

    def inv_load(part):
        at = rows(jnp.where(k == 0, (part + 4) % 8, part), 256)
        return pltpu.make_async_copy(inv_hbm.at[0, at], inv_v.at[at], load_sem.at[part])

    rhs_load = pltpu.make_async_copy(rhs_hbm.at[0], rhs_v, load_sem.at[8])
    cpl_load = pltpu.make_async_copy(cpl_hbm.at[0], cpl_v, load_sem.at[9])
    rinv_load = pltpu.make_async_copy(rinv_hbm, rinv_v, load_sem.at[10])
    root_load = pltpu.make_async_copy(root_hbm, root_v, load_sem.at[11])
    counts_load = pltpu.make_async_copy(counts_hbm, counts, load_sem.at[12])
    map_load = pltpu.make_async_copy(map_hbm, map_ref, load_sem.at[13])
    counts_load.start()
    rhs_load.start()
    for part in range(8):
        inv_load(part).start()
    map_load.start()
    cpl_load.start()
    rinv_load.start()
    root_load.start()

    barrier = pltpu.get_barrier_semaphore()
    pl.semaphore_signal(barrier, inc=1, device_id=sib, device_id_type=MESH)
    for d in range(1, NZ):
        pl.semaphore_signal(barrier, inc=1, device_id=zdev(d), device_id_type=MESH)
    for e in range(1, NXY):
        pl.semaphore_signal(barrier, inc=1, device_id=xydev(e // 4, e % 4), device_id_type=MESH)


    counts_load.wait()
    count = counts[f]
    own = k * 8 + z
    rhs_load.wait()
    spot = c * 512 + lax.broadcasted_iota(jnp.int32, (512, BLK), 0)
    vector = jnp.concatenate(split(jnp.where(spot < count, rhs_v[...], 0.0)), axis=1)
    vec_hl[:512, :] = vector
    vec_hl[512:, :] = vector


    def z_reduce(part, rs, zs, zr):
        def copy(index, src, d):
            return rcopy(src, rs.at[index], zs, zr.at[(0, 0, 1, 2, 2, 2, 2)[index]], zdev(d))

        def send(step):
            index = {0: 0, 1: 1, 2: 2, 5: 3, 6: 4}[step]
            return copy(index, part(zat(step)), {0: 2, 1: 1, 2: -1, 5: 1, 6: -1}[step])

        def arrived(begin, end, sem):
            at = rs.at[pl.ds(begin, end - begin)]
            pltpu.make_async_copy(at, at, zr.at[sem]).wait()

        def relay():
            arrived(0, 2, 0)
            part(chip(2))[...] += rs[0] + rs[1]
            copy(5, part(chip(2)), 2).start()
            arrived(2, 3, 1)
            part(chip(-2))[...] += rs[2]
            copy(6, part(chip(-2)), -2).start()

        def total():
            arrived(3, 7, 2)
            return part(z)[...] + ((rs[3] + rs[4]) + (rs[5] + rs[6]))

        return send, relay, total

    def gather(piece, gs, gr, sr):
        def z_copy(index, d_owner, d):
            at = piece(k, chip(d_owner))
            return rcopy(at, at, gs, gr.at[index], zdev(d))

        def sib_copy(owner):
            at = piece(k, owner)
            return rcopy(at, at, gs, sr.at[owner], sib)

        def sib_arrival(owner):
            at = piece(1 - k, owner)
            return rcopy(at, at, gs, sr.at[owner], sib)

        first = [(0, 0, 2), (1, 0, -2), (2, 0, 1), (3, 0, -1)]
        second = [(4, -2, 1), (5, -2, 2), (6, 2, -1)]
        arrivals = {0: -2, 1: 2, 2: -1, 3: 1, 4: -3, 5: -4, 6: 3}

        def arrive(index):
            z_copy(index, arrivals[index], 1).wait_recv()

        def pass_on(index):
            sib_copy(chip(arrivals[index])).start()

        def start():
            for item in first:
                z_copy(*item).start()
            sib_copy(z).start()

        def relay():
            arrive(0)
            z_copy(*second[0]).start()
            z_copy(*second[1]).start()
            pass_on(0)
            arrive(1)
            z_copy(*second[2]).start()
            pass_on(1)

        def near():
            for index in (2, 3):
                arrive(index)
                pass_on(index)

        def far():
            for index in (6, 4, 5):
                arrive(index)
                pass_on(index)

        def take(begin, end):
            owners = [chip(d) for d in ARRIVALS[begin:end]]
            for owner in owners:
                sib_arrival(owner).wait_recv()
            return owners

        return start, relay, near, far, take

    def z_reduce_direct(part, rs, zs, zr):
        def start():
            for step in range(7):
                rcopy(part(zat(step)), rs.at[step], zs, zr, zdev(far_first(step))).start()

        def total():
            pltpu.make_async_copy(rs, rs, zr).wait()
            value = part(z)[...]
            for step in range(7):
                value = value + rs[step]
            return value

        return start, total

    def gather_direct(piece, gs, gr, sr):
        def z_copy(step, owner):
            at = piece(k, owner)
            return rcopy(at, at, gs, gr.at[step], zdev(far_first(step)))

        def sib_copy(owner):
            at = piece(k, owner)
            return rcopy(at, at, gs, sr, sib)

        def start():
            for step in range(7):
                z_copy(step, z).start()
            sib_copy(z).start()

        def finish():
            for step in (5, 6, 3, 4, 1, 2, 0):
                owner = chip(-far_first(step))
                z_copy(step, owner).wait_recv()
                sib_copy(owner).start()
            await_slabs(sr, NZ)

        return start, finish


    def slab(p):
        return p % 2, rows(p // 2, 8)

    def plane_at(df, dr):
        return slab(((f + df) % 4) * 4 + (r + dr) % 4)

    here = plane_at(0, 0)

    def plane(src, recv, full, ps, pr, qr):
        def out_copy(step):
            df, dr = PLANE[step]
            return rcopy(src.at[plane_at(df, dr)], recv.at[step], ps, pr, xydev(df, dr))

        def all_copy(step):
            df, dr = PLANE[step]
            return rcopy(full.at[here], full.at[here], ps, qr, xydev(df, dr))

        def start():
            for step in range(15):
                out_copy(step).start()

        def middle(combine):
            total = src[here]
            pltpu.make_async_copy(recv, recv, pr).wait()
            for step in range(15):
                total = total + recv[step]
            full[here] = combine(total)
            for step in range(15):
                all_copy(step).start()

        def finish():
            await_slabs(qr, 15)
            return join(full[0], full[1], 1)

        return start, middle, finish


    def forward_group(group):
        steps = range(4 * group, 4 * group + 4)
        for part in ((0, 1), (2, 3), (4, 5, 6, 7), ())[group]:
            inv_load(part).wait()
        highs, lows = [], []
        for step in steps:
            at = rows(block_of(step))
            high, low = split(inv_v[at, :])
            highs.append(high)
            lows.append(low)
        values = []
        for high, low in zip(highs, lows):
            value = mm(join(high, low, 1), vec_hl[...])
            values.append((value[:, :BLK] + value[:, BLK:]).T)
        return values

    core_copy1 = rcopy(part1.at[rows(1 - k, 8)], core1, c1s, c1r, sib)

    for group in range(2):
        for j, value in enumerate(forward_group(group)):
            part1[block_of(4 * group + j)] = value
    pl.semaphore_wait(barrier, NZ + NXY - 1)
    core_copy1.start()

    quarter = [pl.ds((q % 2) * QSRC, QSRC) for q in range(4)]
    sum1 = [
        z_reduce(lambda owner, q=q: part1.at[k * 8 + owner, pl.ds(q * QSRC, QSRC)], rs1.at[q], z1s, z1r.at[q])
        for q in range(4)
    ]
    for group in range(2):
        values = forward_group(group + 2)
        if not group:
            core_copy1.wait_recv()
        for j in range(4):
            owner = zat(4 * group + j)
            part1[k * 8 + owner] = values[j] + core1[owner]
        for step in ((0, 1, 2), (5, 6))[group]:
            for q in (0, 1):
                sum1[q][0](step).start()
    for step in (0, 1, 2, 5, 6):
        for q in (2, 3):
            sum1[q][0](step).start()

    cpl_load.wait()

    def split_cpl(i):
        at = rows(i)
        high, low = split(cpl_v[at, :])
        cpl_hi[at, :] = high
        cpl_lo[at, :] = low

    loop(16, split_cpl)

    def build_map(i):
        at = rows(i)
        spots = i * BLK + lax.broadcasted_iota(jnp.int32, (BLK, 384), 0)
        hot = (map_ref[...] - c * 768 == spots).astype(F32)
        place[at, :] = hot.astype(BF16)
        place_t[i] = hot.T.astype(BF16)

    map_load.wait()
    loop(6, build_map)

    def split_rinv(i):
        at = rows(i)
        value = rinv_v[at, :]
        high, low = split(value)
        rin_hi[at, :] = high
        rin_lo[at, :] = low
        high, low = split(value.T)
        rint_hi[i] = high
        rint_lo[i] = low

    def split_inv(i):
        at = rows(i)
        high, low = split(inv_v[at, :])
        inv_hi[at, :] = high
        inv_lo[at, :] = low

    def turn_cpl(i):
        high, low = split(cpl_v[rows(i), :].T)
        cplt_hi[i] = high
        cplt_lo[i] = low

    root_load.wait()
    for i in range(6):
        turned = root_v[i * BLK:(i + 1) * BLK, :].T
        for h in range(2):
            root_t[h, i // 3, :, (i % 3) * BLK:(i % 3 + 1) * BLK] = turned[h * SRC:(h + 1) * SRC]
    live = r * 2048 + own * BLK + lax.broadcasted_iota(jnp.int32, (QSRC, BLK), 1) < count

    ag1, xy2, ag3, xy4, ag5 = [], [], [], [], []
    for q in range(4):
        sum1[q][1]()
    rinv_load.wait()
    loop(6, split_rinv)
    for q in range(4):
        forward = jnp.where(live, sum1[q][2](), 0.0)
        fwd[q // 2, quarter[q], :] = forward
        full1[q // 2, own, quarter[q], :] = forward
        ag1.append(gather(
            lambda kk, zz, q=q: full1.at[q // 2, kk * 8 + zz, quarter[q]], g1s, g1r.at[q], s1r.at[q]
        ))
        ag1[q][0]()

    def use_border(h):
        def use(owners):
            blocks = [side * 8 + owner for owner in owners for side in (k, 1 - k)]
            left = stack(jnp.concatenate([full1[h, block] for block in blocks], axis=1))
            high = jnp.concatenate([cpl_hi[rows(block), :] for block in blocks], axis=0)
            low = jnp.concatenate([cpl_lo[rows(block), :] for block in blocks], axis=0)
            return mm_split(left, high, low)

        return use

    for q in range(4):
        ag1[q][1]()
    for q in range(4):
        ag1[q][2]()
    for h in range(2):
        for q in (2 * h, 2 * h + 1):
            ag1[q][3]()
        owners = [ag1[q][4](0, 4) for q in (2 * h, 2 * h + 1)][0]
        acc_b[...] = use_border(h)(owners)
        owners = [ag1[q][4](4, 8) for q in (2 * h, 2 * h + 1)][0]
        whole = halves(acc_b[...] + use_border(h)(owners))
        border_hl = stack(whole)
        spread = halves(mm(border_hl, jnp.concatenate([place_t[i] for i in range(6)], axis=1)))
        spread_s[h, 0] = spread[:, :384]
        spread_s[h, 1] = spread[:, 384:]
        xy2.append(plane(
            spread_s.at[h], xyr2.at[h], upd_t.at[h], p2s, p2r.at[h], q2r.at[h]
        ))
        xy2[h][0]()

    loop(8, turn_cpl)
    for h in range(2):
        xy2[h][1](lambda total, h=h: root_t.at[h][here] - total)

    def core_copy3(h):
        return rcopy(
            part3.at[h, 1 - k], core3.at[h], c3s, c3r.at[h], sib
        )

    def slab3(kk, zz):
        return kk, rows(zz, 8)

    loop(8, lambda i: turn_cpl(i + 8))
    sum3 = []
    for h in range(2):
        upd_hl = stack(xy2[h][2]())
        for side in (1 - k, k):
            blocks = [side * 3 + i for i in range(3)]
            part3[h, side] = halves(
                mm_split(
                    upd_hl,
                    jnp.concatenate([rint_hi[block] for block in blocks], axis=1),
                    jnp.concatenate([rint_lo[block] for block in blocks], axis=1),
                )
            )
            if side is not k:
                core_copy3(h).start()
        core_copy3(h).wait_recv()
        part3[h, k] += core3[h]
        sum3.append(z_reduce_direct(
            lambda owner, h=h: part3.at[h].at[slab3(k, owner)], rs3.at[h], z3s, z3r.at[h]
        ))
        sum3[h][0]()
    loop(16, split_inv)
    for h in range(2):
        full3.at[h][slab3(k, z)] = sum3[h][1]()
        ag3.append(gather_direct(
            lambda kk, zz, h=h: full3.at[h].at[slab3(kk, zz)], g3s, g3r.at[h], s3r.at[h]
        ))
        ag3[h][0]()

    for h in range(2):
        ag3[h][1]()
        fwd_hl = stack(join(full3[h, 0], full3[h, 1], 1))
        value = halves(mm_split(fwd_hl, rin_hi[...], rin_lo[...]))
        back_s[h, 0] = value[:, :384]
        back_s[h, 1] = value[:, 384:]
        xy4.append(plane(
            back_s.at[h], xyr4.at[h], back_t.at[h], p4s, p4r.at[h], q4r.at[h]
        ))
        xy4[h][0]()
    for h in range(2):
        xy4[h][1](lambda total: total)

    def core_copy5(h, group):
        src = part5.at[h, rows(2 * (1 - k) + group, 4)]
        return rcopy(src, core5.at[h, pl.ds(4 * group, 4)], c5s, c5r.at[h], sib)

    sum5 = []
    for h in range(2):
        back = xy4[h][2]()
        left = stack(halves(mm(stack(back), place[...])))

        def correction_group(group, left=left):
            blocks = [block_of(step) for step in range(4 * group, 4 * group + 4)]
            value = halves(
                mm_split(
                    left,
                    jnp.concatenate([cplt_hi[block] for block in blocks], axis=1),
                    jnp.concatenate([cplt_lo[block] for block in blocks], axis=1),
                )
            )
            return [value[:, j * BLK:(j + 1) * BLK] for j in range(4)]

        for group in range(2):
            for j, value in enumerate(correction_group(group)):
                part5[h, block_of(4 * group + j)] = value
            core_copy5(h, group).start()
        for q in (2 * h, 2 * h + 1):
            sum5.append(z_reduce(
                lambda owner, q=q: part5.at[q // 2, k * 8 + owner, quarter[q]], rs5.at[q], z5s, z5r.at[q]
            ))
        values = correction_group(2) + correction_group(3)
        for step in range(8):
            part5[h, block_of(step + 8)] = values[step]
        pltpu.make_async_copy(core5.at[h], core5.at[h], c5r.at[h]).wait()
        for step in range(8):
            owner = zat(step)
            part5[h, k * 8 + owner] += core5[h, owner]
            if step in (0, 1, 2, 5, 6):
                for q in (2 * h, 2 * h + 1):
                    sum5[q][0](step).start()

    for i in range(6):
        half, at = i // 3, (i % 3) * BLK
        root_v[i * BLK:(i + 1) * BLK, :] = join(back_t[0, half, :, at:at + BLK], back_t[1, half, :, at:at + BLK], 0).T
    root_store = pltpu.make_async_copy(root_v, root_out, out_sem.at[0])
    root_store.start()

    for q in range(4):
        sum5[q][1]()
    for q in range(4):
        rest = fwd[q // 2, quarter[q], :] - sum5[q][2]()
        full5[q // 2, own, quarter[q], :] = jnp.where(live, rest, 0.0)
        ag5.append(gather(
            lambda kk, zz, q=q: full5.at[q // 2, kk * 8 + zz, quarter[q]], g5s, g5r.at[q], s5r.at[q]
        ))
        ag5[q][0]()

    def yslab(d):
        return rows((r + d) % 4, 16)

    def ydev(d):
        return (f, (r + d) % 4, c)

    def y_copy(h, d):
        return rcopy(ypart.at[h, yslab(d)], yrs.at[h, d - 1], y6s, y6r.at[h], ydev(d))

    def w_copy(h, d):
        return rcopy(yfull.at[h, yslab(0)], yfull.at[h, yslab(0)], y6s, w6r.at[h], ydev(d))

    def use_back(h):
        def use(owners):
            blocks = [side * 8 + owner for owner in owners for side in (k, 1 - k)]
            left = stack(jnp.concatenate([full5[h, block] for block in blocks], axis=1))
            high = jnp.concatenate([inv_hi[rows(block), :] for block in blocks], axis=0)
            low = jnp.concatenate([inv_lo[rows(block), :] for block in blocks], axis=0)
            return mm_split(left, high, low)

        return use

    for q in range(4):
        ag5[q][1]()
    for q in range(4):
        ag5[q][2]()
    for h in range(2):
        for q in (2 * h, 2 * h + 1):
            ag5[q][3]()
        owners = [ag5[q][4](0, 4) for q in (2 * h, 2 * h + 1)][0]
        acc_c[...] = use_back(h)(owners)
        owners = [ag5[q][4](4, 8) for q in (2 * h, 2 * h + 1)][0]
        whole = halves(acc_c[...] + use_back(h)(owners))
        ypart[h] = whole
        for d in (2, 1, 3):
            y_copy(h, d).start()
    for h in range(2):
        total = ypart[h, yslab(0)]
        pltpu.make_async_copy(yrs.at[h], yrs.at[h], y6r.at[h]).wait()
        for d in (1, 3, 2):
            total = total + yrs[h, d - 1]
        yfull[h, yslab(0)] = total
        for d in (2, 1, 3):
            w_copy(h, d).start()
    for h in range(2):
        await_blocks(w6r.at[h], 3)
    for i in range(4):
        at = c * 512 + i * BLK + lax.broadcasted_iota(jnp.int32, (BLK, BLK), 0)
        value = join(yfull[0, :, i * BLK:(i + 1) * BLK], yfull[1, :, i * BLK:(i + 1) * BLK], 0).T
        rhs_v[i * BLK:(i + 1) * BLK, :] = jnp.where(at < count, value, 0.0)
    child_store = pltpu.make_async_copy(rhs_v, child_out.at[0], out_sem.at[1])
    child_store.start()
    await_blocks(c1s, 8 * 2)
    await_blocks(z1s, 2 * 7)
    await_blocks(g1s, 2 * 15)
    await_slabs(p2s, 2 * 30)
    await_slabs(c3s, 2 * 8)
    await_slabs(z3s, 2 * 7)
    await_slabs(g3s, 2 * 15)
    await_slabs(p4s, 2 * 30)
    await_blocks(c5s, 2 * 8)
    await_blocks(z5s, 2 * 7)
    await_blocks(g5s, 2 * 15)
    await_blocks(y6s, 2 * 6)
    root_store.wait()
    child_store.wait()


def hand_over(child, root, child_out, root_out, child_v, root_v, sems):
    loads = [
        pltpu.make_async_copy(child, child_v, sems.at[0]),
        pltpu.make_async_copy(root, root_v, sems.at[1]),
    ]
    stores = [
        pltpu.make_async_copy(child_v, child_out, sems.at[2]),
        pltpu.make_async_copy(root_v, root_out, sems.at[3]),
    ]
    for load in loads:
        load.start()
    for load, store in zip(loads, stores):
        load.wait()
        store.start()
    for store in stores:
        store.wait()


def per_device(child_rhs, root_rhs, child_inv, coupling, root_inv, pivot_counts, border_map):
    def v(*shape, dtype=F32):
        return pltpu.VMEM(shape, dtype)

    dma = pltpu.SemaphoreType.DMA
    scratch = [
        v(512, 128), v(768, 128), v(2048, 512), v(2048, 384), v(768, 768),
        v(2048, 512, dtype=BF16), v(2048, 512, dtype=BF16), v(2048, 384, dtype=BF16), v(2048, 384, dtype=BF16),
        v(768, 768, dtype=BF16), v(768, 768, dtype=BF16),
        v(1024, 256, dtype=BF16), v(768, 384, dtype=BF16), v(6, 384, 128, dtype=BF16),
        v(16, 384, 128, dtype=BF16), v(16, 384, 128, dtype=BF16),
        v(6, 768, 128, dtype=BF16), v(6, 768, 128, dtype=BF16), v(2, 2, 64, 384), v(2, 64, 128),
        v(16, 128, 128), v(8, 128, 128), v(4, 7, 32, 128), v(2, 16, 64, 128),
        v(2, 16, 64, 128), v(2, 8, 64, 128), v(4, 7, 32, 128), v(2, 16, 64, 128),
        v(2, 2, 64, 384), v(2, 15, 8, 384), v(2, 2, 64, 384),
        v(2, 2, 64, 384), v(2, 64, 384), v(2, 7, 8, 384), v(2, 2, 64, 384),
        v(2, 2, 64, 384), v(2, 15, 8, 384), v(2, 2, 64, 384),
        v(128, 384), v(128, 512),
        v(2, 64, 512), v(2, 3, 16, 512), v(2, 64, 512),
        pltpu.SMEM((4,), jnp.int32), pltpu.VMEM((1, 384), jnp.int32), dma((14,)), dma((2,)),
    ]
    scratch += [dma] * 12
    scratch += [dma, dma((4, 3)), dma((4, 7)), dma((4, 8))]
    scratch += [dma((2,)), dma((2,)), dma((2, 7)), dma((2,))]
    scratch += [dma((2,)), dma((4, 3)), dma((4, 7)), dma((4, 8))]
    scratch += [dma((2,))] * 6
    hbm = pl.BlockSpec(memory_space=pl.ANY)
    results = tuple(
        pl.pallas_call(
            kernel,
            out_shape=(
                jax.ShapeDtypeStruct((1, 512, 128), F32),
                jax.ShapeDtypeStruct((768, 128), F32),
            ),
            in_specs=[hbm] * 7,
            out_specs=(hbm, hbm),
            scratch_shapes=scratch,
            compiler_params=pltpu.CompilerParams(
                collective_id=0, has_side_effects=True, vmem_limit_bytes=56 << 20
            ),
            cost_estimate=pl.CostEstimate(flops=5 * 10**9, bytes_accessed=11 * 10**6, transcendentals=0),
        )(child_rhs, root_rhs, child_inv, coupling, root_inv, pivot_counts, border_map)
    )
    return tuple(
        pl.pallas_call(
            hand_over,
            out_shape=tuple(jax.ShapeDtypeStruct(a.shape, a.dtype) for a in results),
            in_specs=[hbm] * 2,
            out_specs=(hbm, hbm),
            scratch_shapes=[v(1, 512, 128), v(768, 128), dma((4,))],
            compiler_params=pltpu.CompilerParams(vmem_limit_bytes=56 << 20),
        )(*results)
    )


def solution(mesh):
    in_specs = (
        P("front", "col", None),
        P("col", None),
        P("front", "row", "col"),
        P("front", "row", "col"),
        P(("front", "row"), "col"),
        P(),
        P("front", "col"),
    )
    out_specs = (P("front", "col", None), P("col", None))
    return jax.shard_map(
        per_device, mesh=mesh, in_specs=in_specs, out_specs=out_specs, check_vma=False
    )
```

```python
import jax
import jax.numpy as jnp
from jax import lax
from jax.experimental import pallas as pl
from jax.experimental.pallas import tpu as pltpu
from jax.sharding import PartitionSpec as P

MESH = pl.DeviceIdType.MESH
F32 = jnp.float32
BF16 = jnp.bfloat16
NZ = 8
NXY = 16
BLK = 128
SRC = 64
QSRC = 32
PLANE = (
    (2, 2), (2, 1), (2, 3), (1, 2), (3, 2), (2, 0), (0, 2), (1, 1),
    (3, 3), (1, 3), (3, 1), (0, 1), (0, 3), (1, 0), (3, 0),
)
ARRIVALS = (0, -2, 2, -1, 1, 3, -3, -4)


def split(value):
    high = value.astype(BF16)
    low = (value - high.astype(F32)).astype(BF16)
    return high, low


def stack(value):
    return jnp.concatenate(split(value), axis=0)


def mm(left, right):
    return jnp.dot(left, right, preferred_element_type=F32)


def mm_split(left, high, low):
    return mm(jnp.concatenate([left, left], axis=1), jnp.concatenate([high, low], axis=0))


def halves(value):
    rows = value.shape[0] // 2
    return value[:rows] + value[rows:]


def join(left, right, axis):
    return jnp.concatenate([left, right], axis=axis)


def far_first(step):
    return 4 + (1 - 2 * (step % 2)) * ((step + 1) // 2)


def loop(n, body):
    def step(i, carry):
        body(i)
        return carry

    lax.fori_loop(0, n, step, 0)


def rows(block, size=BLK):
    return pl.ds(pl.multiple_of(block * size, size), size)


def kernel(
    rhs_hbm, root_hbm, inv_hbm, cpl_hbm, rinv_hbm, counts_hbm, map_hbm,
    child_out, root_out,
    rhs_v, root_v, inv_v, cpl_v, rinv_v,
    inv_hi, inv_lo, cpl_hi, cpl_lo, rin_hi, rin_lo,
    vec_hl, place, place_t, cplt_hi, cplt_lo, rint_hi, rint_lo, root_t, fwd,
    part1, core1, rs1, full1,
    part5, core5, rs5, full5,
    spread_s, xyr2, upd_t,
    part3, core3, rs3, full3,
    back_s, xyr4, back_t,
    acc_b, acc_c,
    ypart, yrs, yfull,
    counts, map_ref, load_sem, out_sem,
    sent1, sent3, sent5,
    c1r, z1r, g1r, s1r, c3r, z3r, g3r, s3r, c5r, z5r, g5r, s5r,
    p2r, q2r, p4r, q4r, y6r, w6r,
):
    f = lax.axis_index("front")
    r = lax.axis_index("row")
    c = lax.axis_index("col")
    z = c // 2
    k = c % 2
    sib = (f, r, z * 2 + (1 - k))

    way = 1 - 2 * k

    def chip(d):
        return (z + way * d + 2 * NZ) % NZ

    def zdev(d):
        return (f, r, chip(d) * 2 + k)

    def xydev(df, dr):
        return ((f + df) % 4, (r + dr) % 4, c)

    def rcopy(src, dst, ss, rs, dev):
        return pltpu.make_async_remote_copy(
            src_ref=src, dst_ref=dst, send_sem=ss, recv_sem=rs, device_id=dev, device_id_type=MESH
        )

    def await_blocks(sem, count):
        at = inv_v.at[pl.ds(0, count * 16)]
        pltpu.make_async_copy(at, at, sem).wait()

    def await_quarters(sem, count):
        at = inv_v.at[pl.ds(0, count * 8)]
        pltpu.make_async_copy(at, at, sem).wait()

    def await_slabs(sem, count):
        at = cpl_v.at[pl.ds(0, count * 8)]
        pltpu.make_async_copy(at, at, sem).wait()

    def zat(step):
        return chip(far_first(step))

    def block_of(step):
        return (1 - k) * 8 + step if step < 8 else k * 8 + zat(step - 8)

    def inv_load(part):
        at = rows(jnp.where(k == 0, (part + 4) % 8, part), 256)
        return pltpu.make_async_copy(inv_hbm.at[0, at], inv_v.at[at], load_sem.at[(0, 0, 1, 1, 2, 2, 2, 2)[part]])

    rhs_load = pltpu.make_async_copy(rhs_hbm.at[0], rhs_v, load_sem.at[3])
    cpl_load = pltpu.make_async_copy(cpl_hbm.at[0], cpl_v, load_sem.at[4])
    rinv_load = pltpu.make_async_copy(rinv_hbm, rinv_v, load_sem.at[5])
    root_load = pltpu.make_async_copy(root_hbm, root_v, load_sem.at[6])
    counts_load = pltpu.make_async_copy(counts_hbm, counts, load_sem.at[7])
    map_load = pltpu.make_async_copy(map_hbm, map_ref, load_sem.at[8])
    counts_load.start()
    for i in range(4):
        at = pl.ds(i * BLK, BLK)
        pltpu.make_async_copy(rhs_hbm.at[0, at], rhs_v.at[at], load_sem.at[3]).start()
    for part in range(8):
        inv_load(part).start()
    map_load.start()
    cpl_load.start()
    rinv_load.start()
    root_load.start()

    barrier = pltpu.get_barrier_semaphore()
    pl.semaphore_signal(barrier, inc=1, device_id=sib, device_id_type=MESH)
    for d in range(1, NZ):
        pl.semaphore_signal(barrier, inc=1, device_id=zdev(d), device_id_type=MESH)
    for e in range(1, NXY):
        pl.semaphore_signal(barrier, inc=1, device_id=xydev(e // 4, e % 4), device_id_type=MESH)


    counts_load.wait()
    count = counts[f]
    own = k * 8 + z
    rhs_load.wait()
    spot = c * 512 + lax.broadcasted_iota(jnp.int32, (512, BLK), 0)
    vector = jnp.concatenate(split(jnp.where(spot < count, rhs_v[...], 0.0)), axis=1)
    vec_hl[:512, :] = vector
    vec_hl[512:, :] = vector


    def z_reduce(part, rs, zs, zr):
        def copy(index, src, d):
            return rcopy(src, rs.at[index], zs, zr.at[(0, 0, 1, 2, 2, 2, 2)[index]], zdev(d))

        def send(step):
            index = {0: 0, 1: 1, 2: 2, 5: 3, 6: 4}[step]
            return copy(index, part(zat(step)), {0: 2, 1: 1, 2: -1, 5: 1, 6: -1}[step])

        def arrived(begin, end, sem):
            at = rs.at[pl.ds(begin, end - begin)]
            pltpu.make_async_copy(at, at, zr.at[sem]).wait()

        def relay():
            arrived(0, 2, 0)
            part(chip(2))[...] += rs[0] + rs[1]
            copy(5, part(chip(2)), 2).start()
            arrived(2, 3, 1)
            part(chip(-2))[...] += rs[2]
            copy(6, part(chip(-2)), -2).start()

        def total():
            arrived(3, 7, 2)
            return part(z)[...] + ((rs[3] + rs[4]) + (rs[5] + rs[6]))

        return send, relay, total

    def gather(piece, gs, gr, sr):
        def z_copy(index, d_owner, d):
            at = piece(k, chip(d_owner))
            return rcopy(at, at, gs, gr.at[(0, 1, 2, 2, 3, 4, 5)[index]], zdev(d))

        def sib_copy(owner, far):
            at = piece(k, owner)
            return rcopy(at, at, gs, sr.at[far], sib)

        first = [(0, 0, 2), (1, 0, -2), (2, 0, 1), (3, 0, -1)]
        second = [(4, -2, 1), (5, -2, 2), (6, 2, -1)]
        arrivals = {0: -2, 1: 2, 2: -1, 3: 1, 4: -3, 5: -4, 6: 3}

        def arrive(index):
            z_copy(index, arrivals[index], 1).wait_recv()

        def pass_on(index):
            sib_copy(chip(arrivals[index]), index // 4).start()

        def start():
            for item in first:
                z_copy(*item).start()
            sib_copy(z, 0).start()

        def relay():
            arrive(0)
            z_copy(*second[0]).start()
            z_copy(*second[1]).start()
            pass_on(0)
            arrive(1)
            z_copy(*second[2]).start()
            pass_on(1)

        def near():
            await_quarters(gr.at[2], 2)
            for index in (2, 3):
                pass_on(index)

        def far():
            for index in (6, 4, 5):
                arrive(index)
                pass_on(index)

        def take(far):
            await_quarters(sr.at[far], (5, 3)[far])
            return [chip(d) for d in (ARRIVALS[:5], ARRIVALS[5:])[far]]

        return start, relay, near, far, take

    def z_reduce_direct(part, rs, zs, zr):
        def start():
            for step in range(7):
                rcopy(part(zat(step)), rs.at[step], zs, zr, zdev(far_first(step))).start()

        def total():
            pltpu.make_async_copy(rs, rs, zr).wait()
            value = part(z)[...]
            for step in range(7):
                value = value + rs[step]
            return value

        return start, total

    def gather_direct(piece, gs, gr, sr):
        def z_copy(step, owner):
            at = piece(k, owner)
            return rcopy(at, at, gs, gr.at[step], zdev(far_first(step)))

        def sib_copy(owner):
            at = piece(k, owner)
            return rcopy(at, at, gs, sr, sib)

        def start():
            for step in range(7):
                z_copy(step, z).start()
            sib_copy(z).start()

        def finish():
            for step in (5, 6, 3, 4, 1, 2, 0):
                owner = chip(-far_first(step))
                z_copy(step, owner).wait_recv()
                sib_copy(owner).start()
            await_slabs(sr, NZ)

        return start, finish


    def slab(p):
        return p % 2, rows(p // 2, 8)

    def plane_at(df, dr):
        return slab(((f + df) % 4) * 4 + (r + dr) % 4)

    here = plane_at(0, 0)

    def plane(src, recv, full, ps, pr, qr):
        def out_copy(step):
            df, dr = PLANE[step]
            return rcopy(src.at[plane_at(df, dr)], recv.at[step], ps, pr, xydev(df, dr))

        def all_copy(step):
            df, dr = PLANE[step]
            return rcopy(full.at[here], full.at[here], ps, qr, xydev(df, dr))

        def start():
            for step in range(15):
                out_copy(step).start()

        def middle(combine):
            total = src[here]
            pltpu.make_async_copy(recv, recv, pr).wait()
            for step in range(15):
                total = total + recv[step]
            full[here] = combine(total)
            for step in range(15):
                all_copy(step).start()

        def finish():
            await_slabs(qr, 15)
            return join(full[0], full[1], 1)

        return start, middle, finish


    def forward_group(group):
        steps = range(4 * group, 4 * group + 4)
        if group < 3:
            at = inv_v.at[pl.ds(0, (512, 512, 1024)[group])]
            pltpu.make_async_copy(at, at, load_sem.at[group]).wait()
        highs, lows = [], []
        for step in steps:
            at = rows(block_of(step))
            high, low = split(inv_v[at, :])
            highs.append(high)
            lows.append(low)
        values = []
        for high, low in zip(highs, lows):
            value = mm(join(high, low, 1), vec_hl[...])
            values.append((value[:, :BLK] + value[:, BLK:]).T)
        return values

    core_copy1 = rcopy(part1.at[rows(1 - k, 8)], core1, sent1, c1r, sib)

    for group in range(2):
        for j, value in enumerate(forward_group(group)):
            part1[block_of(4 * group + j)] = value
    pl.semaphore_wait(barrier, NZ + NXY - 1)
    core_copy1.start()

    quarter = [pl.ds((q % 2) * QSRC, QSRC) for q in range(4)]
    sum1 = [
        z_reduce(lambda owner, q=q: part1.at[k * 8 + owner, pl.ds(q * QSRC, QSRC)], rs1.at[q], sent1, z1r.at[q])
        for q in range(4)
    ]
    for group in range(2):
        values = forward_group(group + 2)
        if not group:
            core_copy1.wait_recv()
        for j in range(4):
            owner = zat(4 * group + j)
            part1[k * 8 + owner] = values[j] + core1[owner]
        for step in ((0, 1, 2), (5, 6))[group]:
            for q in (0, 1):
                sum1[q][0](step).start()
    for step in (0, 1, 2, 5, 6):
        for q in (2, 3):
            sum1[q][0](step).start()

    cpl_load.wait()

    def split_cpl(i):
        at = rows(i)
        high, low = split(cpl_v[at, :])
        cpl_hi[at, :] = high
        cpl_lo[at, :] = low

    loop(16, split_cpl)

    def build_map(i):
        at = rows(i)
        spots = i * BLK + lax.broadcasted_iota(jnp.int32, (BLK, 384), 0)
        hot = (map_ref[...] - c * 768 == spots).astype(F32)
        place[at, :] = hot.astype(BF16)
        place_t[i] = hot.T.astype(BF16)

    map_load.wait()
    loop(6, build_map)

    def split_rinv(i):
        at = rows(i)
        value = rinv_v[at, :]
        high, low = split(value)
        rin_hi[at, :] = high
        rin_lo[at, :] = low
        high, low = split(value.T)
        rint_hi[i] = high
        rint_lo[i] = low

    def split_inv(i):
        at = rows(i)
        high, low = split(inv_v[at, :])
        inv_hi[at, :] = high
        inv_lo[at, :] = low

    def turn_cpl(i):
        high, low = split(cpl_v[rows(i), :].T)
        cplt_hi[i] = high
        cplt_lo[i] = low

    root_load.wait()
    for i in range(6):
        turned = root_v[i * BLK:(i + 1) * BLK, :].T
        for h in range(2):
            root_t[h, i // 3, :, (i % 3) * BLK:(i % 3 + 1) * BLK] = turned[h * SRC:(h + 1) * SRC]
    live = r * 2048 + own * BLK + lax.broadcasted_iota(jnp.int32, (QSRC, BLK), 1) < count

    ag1, xy2, ag3, xy4, ag5 = [], [], [], [], []
    for q in range(4):
        sum1[q][1]()
    rinv_load.wait()
    loop(6, split_rinv)
    for q in range(4):
        forward = jnp.where(live, sum1[q][2](), 0.0)
        fwd[q // 2, quarter[q], :] = forward
        full1[q // 2, own, quarter[q], :] = forward
        ag1.append(gather(
            lambda kk, zz, q=q: full1.at[q // 2, kk * 8 + zz, quarter[q]], sent1, g1r.at[q], s1r.at[q]
        ))
        ag1[q][0]()

    def use_border(h):
        def use(owners):
            blocks = [side * 8 + owner for owner in owners for side in (k, 1 - k)]
            left = stack(jnp.concatenate([full1[h, block] for block in blocks], axis=1))
            high = jnp.concatenate([cpl_hi[rows(block), :] for block in blocks], axis=0)
            low = jnp.concatenate([cpl_lo[rows(block), :] for block in blocks], axis=0)
            return mm_split(left, high, low)

        return use

    for q in range(4):
        ag1[q][1]()
    for q in range(4):
        ag1[q][2]()
    for h in range(2):
        for q in (2 * h, 2 * h + 1):
            ag1[q][3]()
        owners = [ag1[q][4](0) for q in (2 * h, 2 * h + 1)][0]
        acc_b[...] = use_border(h)(owners)
        owners = [ag1[q][4](1) for q in (2 * h, 2 * h + 1)][0]
        whole = halves(acc_b[...] + use_border(h)(owners))
        border_hl = stack(whole)
        spread = halves(mm(border_hl, jnp.concatenate([place_t[i] for i in range(6)], axis=1)))
        spread_s[h, 0] = spread[:, :384]
        spread_s[h, 1] = spread[:, 384:]
        xy2.append(plane(
            spread_s.at[h], xyr2.at[h], upd_t.at[h], sent3, p2r.at[h], q2r.at[h]
        ))
        xy2[h][0]()

    loop(8, turn_cpl)
    for h in range(2):
        xy2[h][1](lambda total, h=h: root_t.at[h][here] - total)

    def core_copy3(h):
        return rcopy(
            part3.at[h, 1 - k], core3.at[h], sent3, c3r.at[h], sib
        )

    def slab3(kk, zz):
        return kk, rows(zz, 8)

    loop(8, lambda i: turn_cpl(i + 8))
    sum3 = []
    for h in range(2):
        upd_hl = stack(xy2[h][2]())
        for side in (1 - k, k):
            blocks = [side * 3 + i for i in range(3)]
            part3[h, side] = halves(
                mm_split(
                    upd_hl,
                    jnp.concatenate([rint_hi[block] for block in blocks], axis=1),
                    jnp.concatenate([rint_lo[block] for block in blocks], axis=1),
                )
            )
            if side is not k:
                core_copy3(h).start()
        core_copy3(h).wait_recv()
        part3[h, k] += core3[h]
        sum3.append(z_reduce_direct(
            lambda owner, h=h: part3.at[h].at[slab3(k, owner)], rs3.at[h], sent3, z3r.at[h]
        ))
        sum3[h][0]()
    loop(16, split_inv)
    for h in range(2):
        full3.at[h][slab3(k, z)] = sum3[h][1]()
        ag3.append(gather_direct(
            lambda kk, zz, h=h: full3.at[h].at[slab3(kk, zz)], sent3, g3r.at[h], s3r.at[h]
        ))
        ag3[h][0]()

    for h in range(2):
        ag3[h][1]()
        fwd_hl = stack(join(full3[h, 0], full3[h, 1], 1))
        value = halves(mm_split(fwd_hl, rin_hi[...], rin_lo[...]))
        back_s[h, 0] = value[:, :384]
        back_s[h, 1] = value[:, 384:]
        xy4.append(plane(
            back_s.at[h], xyr4.at[h], back_t.at[h], sent3, p4r.at[h], q4r.at[h]
        ))
        xy4[h][0]()
    for h in range(2):
        xy4[h][1](lambda total: total)

    def core_copy5(h, group):
        src = part5.at[h, rows(2 * (1 - k) + group, 4)]
        return rcopy(src, core5.at[h, pl.ds(4 * group, 4)], sent5, c5r.at[h], sib)

    sum5 = []
    for h in range(2):
        back = xy4[h][2]()
        left = stack(halves(mm(stack(back), place[...])))

        def correction_group(group, left=left):
            blocks = [block_of(step) for step in range(4 * group, 4 * group + 4)]
            value = halves(
                mm_split(
                    left,
                    jnp.concatenate([cplt_hi[block] for block in blocks], axis=1),
                    jnp.concatenate([cplt_lo[block] for block in blocks], axis=1),
                )
            )
            return [value[:, j * BLK:(j + 1) * BLK] for j in range(4)]

        for group in range(2):
            for j, value in enumerate(correction_group(group)):
                part5[h, block_of(4 * group + j)] = value
            core_copy5(h, group).start()
        for q in (2 * h, 2 * h + 1):
            sum5.append(z_reduce(
                lambda owner, q=q: part5.at[q // 2, k * 8 + owner, quarter[q]], rs5.at[q], sent5, z5r.at[q]
            ))
        values = correction_group(2) + correction_group(3)
        for step in range(8):
            part5[h, block_of(step + 8)] = values[step]
        pltpu.make_async_copy(core5.at[h], core5.at[h], c5r.at[h]).wait()
        for step in range(8):
            owner = zat(step)
            part5[h, k * 8 + owner] += core5[h, owner]
            if step in (0, 1, 2, 5, 6):
                for q in (2 * h, 2 * h + 1):
                    sum5[q][0](step).start()

    for i in range(6):
        half, at = i // 3, (i % 3) * BLK
        root_v[i * BLK:(i + 1) * BLK, :] = join(back_t[0, half, :, at:at + BLK], back_t[1, half, :, at:at + BLK], 0).T
    root_store = pltpu.make_async_copy(root_v, root_out, out_sem.at[0])
    root_store.start()

    for q in range(4):
        sum5[q][1]()
    for q in range(4):
        rest = fwd[q // 2, quarter[q], :] - sum5[q][2]()
        full5[q // 2, own, quarter[q], :] = jnp.where(live, rest, 0.0)
        ag5.append(gather(
            lambda kk, zz, q=q: full5.at[q // 2, kk * 8 + zz, quarter[q]], sent5, g5r.at[q], s5r.at[q]
        ))
        ag5[q][0]()

    def yslab(d):
        return rows((r + d) % 4, 16)

    def ydev(d):
        return (f, (r + d) % 4, c)

    def y_copy(h, d):
        return rcopy(ypart.at[h, yslab(d)], yrs.at[h, d - 1], sent5, y6r.at[h], ydev(d))

    def w_copy(h, d):
        return rcopy(yfull.at[h, yslab(0)], yfull.at[h, yslab(0)], sent5, w6r.at[h], ydev(d))

    def use_back(h):
        def use(owners):
            blocks = [side * 8 + owner for owner in owners for side in (k, 1 - k)]
            left = stack(jnp.concatenate([full5[h, block] for block in blocks], axis=1))
            high = jnp.concatenate([inv_hi[rows(block), :] for block in blocks], axis=0)
            low = jnp.concatenate([inv_lo[rows(block), :] for block in blocks], axis=0)
            return mm_split(left, high, low)

        return use

    for q in range(4):
        ag5[q][1]()
    for q in range(4):
        ag5[q][2]()
    for h in range(2):
        for q in (2 * h, 2 * h + 1):
            ag5[q][3]()
        owners = [ag5[q][4](0) for q in (2 * h, 2 * h + 1)][0]
        acc_c[...] = use_back(h)(owners)
        owners = [ag5[q][4](1) for q in (2 * h, 2 * h + 1)][0]
        whole = halves(acc_c[...] + use_back(h)(owners))
        ypart[h] = whole
        for d in (2, 1, 3):
            y_copy(h, d).start()
    for h in range(2):
        total = ypart[h, yslab(0)]
        pltpu.make_async_copy(yrs.at[h], yrs.at[h], y6r.at[h]).wait()
        for d in (1, 3, 2):
            total = total + yrs[h, d - 1]
        yfull[h, yslab(0)] = total
        for d in (2, 1, 3):
            w_copy(h, d).start()
    for h in range(2):
        await_blocks(w6r.at[h], 3)
    for i in range(4):
        at = c * 512 + i * BLK + lax.broadcasted_iota(jnp.int32, (BLK, BLK), 0)
        value = join(yfull[0, :, i * BLK:(i + 1) * BLK], yfull[1, :, i * BLK:(i + 1) * BLK], 0).T
        rhs_v[i * BLK:(i + 1) * BLK, :] = jnp.where(at < count, value, 0.0)
        part = pl.ds(i * BLK, BLK)
        pltpu.make_async_copy(rhs_v.at[part], child_out.at[0, part], out_sem.at[1]).start()
    child_store = pltpu.make_async_copy(rhs_v, child_out.at[0], out_sem.at[1])
    await_blocks(sent1, 8 * 2 + 2 * 7 + 2 * 15)
    await_slabs(sent3, 2 * 30 + 2 * 8 + 2 * 7 + 2 * 15 + 2 * 30)
    await_blocks(sent5, 2 * 8 + 2 * 7 + 2 * 15 + 2 * 6)
    root_store.wait()
    child_store.wait()


def hand_over(child, root, child_out, root_out, child_v, root_v, sems):
    loads = [
        pltpu.make_async_copy(child, child_v, sems.at[0]),
        pltpu.make_async_copy(root, root_v, sems.at[1]),
    ]
    stores = [
        pltpu.make_async_copy(child_v, child_out, sems.at[2]),
        pltpu.make_async_copy(root_v, root_out, sems.at[3]),
    ]
    for load in loads:
        load.start()
    for load, store in zip(loads, stores):
        load.wait()
        store.start()
    for store in stores:
        store.wait()


def per_device(child_rhs, root_rhs, child_inv, coupling, root_inv, pivot_counts, border_map):
    def v(*shape, dtype=F32):
        return pltpu.VMEM(shape, dtype)

    dma = pltpu.SemaphoreType.DMA
    scratch = [
        v(512, 128), v(768, 128), v(2048, 512), v(2048, 384), v(768, 768),
        v(2048, 512, dtype=BF16), v(2048, 512, dtype=BF16), v(2048, 384, dtype=BF16), v(2048, 384, dtype=BF16),
        v(768, 768, dtype=BF16), v(768, 768, dtype=BF16),
        v(1024, 256, dtype=BF16), v(768, 384, dtype=BF16), v(6, 384, 128, dtype=BF16),
        v(16, 384, 128, dtype=BF16), v(16, 384, 128, dtype=BF16),
        v(6, 768, 128, dtype=BF16), v(6, 768, 128, dtype=BF16), v(2, 2, 64, 384), v(2, 64, 128),
        v(16, 128, 128), v(8, 128, 128), v(4, 7, 32, 128), v(2, 16, 64, 128),
        v(2, 16, 64, 128), v(2, 8, 64, 128), v(4, 7, 32, 128), v(2, 16, 64, 128),
        v(2, 2, 64, 384), v(2, 15, 8, 384), v(2, 2, 64, 384),
        v(2, 2, 64, 384), v(2, 64, 384), v(2, 7, 8, 384), v(2, 2, 64, 384),
        v(2, 2, 64, 384), v(2, 15, 8, 384), v(2, 2, 64, 384),
        v(128, 384), v(128, 512),
        v(2, 64, 512), v(2, 3, 16, 512), v(2, 64, 512),
        pltpu.SMEM((4,), jnp.int32), pltpu.VMEM((1, 384), jnp.int32), dma((9,)), dma((2,)),
    ]
    scratch += [dma] * 3
    scratch += [dma, dma((4, 3)), dma((4, 6)), dma((4, 2))]
    scratch += [dma((2,)), dma((2,)), dma((2, 7)), dma((2,))]
    scratch += [dma((2,)), dma((4, 3)), dma((4, 6)), dma((4, 2))]
    scratch += [dma((2,))] * 6
    hbm = pl.BlockSpec(memory_space=pl.ANY)
    results = tuple(
        pl.pallas_call(
            kernel,
            out_shape=(
                jax.ShapeDtypeStruct((1, 512, 128), F32),
                jax.ShapeDtypeStruct((768, 128), F32),
            ),
            in_specs=[hbm] * 7,
            out_specs=(hbm, hbm),
            scratch_shapes=scratch,
            compiler_params=pltpu.CompilerParams(
                collective_id=0, has_side_effects=True, vmem_limit_bytes=56 << 20
            ),
            cost_estimate=pl.CostEstimate(flops=5 * 10**9, bytes_accessed=11 * 10**6, transcendentals=0),
        )(child_rhs, root_rhs, child_inv, coupling, root_inv, pivot_counts, border_map)
    )
    return tuple(
        pl.pallas_call(
            hand_over,
            out_shape=tuple(jax.ShapeDtypeStruct(a.shape, a.dtype) for a in results),
            in_specs=[hbm] * 2,
            out_specs=(hbm, hbm),
            scratch_shapes=[v(1, 512, 128), v(768, 128), dma((4,))],
            compiler_params=pltpu.CompilerParams(vmem_limit_bytes=56 << 20),
        )(*results)
    )


def solution(mesh):
    in_specs = (
        P("front", "col", None),
        P("col", None),
        P("front", "row", "col"),
        P("front", "row", "col"),
        P(("front", "row"), "col"),
        P(),
        P("front", "col"),
    )
    out_specs = (P("front", "col", None), P("col", None))
    return jax.shard_map(
        per_device, mesh=mesh, in_specs=in_specs, out_specs=out_specs, check_vma=False
    )
```

```python
import jax
import jax.numpy as jnp
from jax import lax
from jax.experimental import pallas as pl
from jax.experimental.pallas import tpu as pltpu
from jax.sharding import PartitionSpec as P

MESH = pl.DeviceIdType.MESH
F32 = jnp.float32
BF16 = jnp.bfloat16
NZ = 8
NXY = 16
BLK = 128
SRC = 64
QSRC = 32
PLANE = (
    (2, 2), (2, 1), (2, 3), (1, 2), (3, 2), (2, 0), (0, 2), (1, 1),
    (3, 3), (1, 3), (3, 1), (0, 1), (0, 3), (1, 0), (3, 0),
)
ARRIVALS = (0, -2, 2, -1, 1, 3, -3, -4)


def split(value):
    high = value.astype(BF16)
    low = (value - high.astype(F32)).astype(BF16)
    return high, low


def stack(value):
    return jnp.concatenate(split(value), axis=0)


def mm(left, right):
    return jnp.dot(left, right, preferred_element_type=F32)


def mm_split(left, high, low):
    return mm(jnp.concatenate([left, left], axis=1), jnp.concatenate([high, low], axis=0))


def halves(value):
    rows = value.shape[0] // 2
    return value[:rows] + value[rows:]


def join(left, right, axis):
    return jnp.concatenate([left, right], axis=axis)


def far_first(step):
    return 4 + (1 - 2 * (step % 2)) * ((step + 1) // 2)


def loop(n, body):
    def step(i, carry):
        body(i)
        return carry

    lax.fori_loop(0, n, step, 0)


def rows(block, size=BLK):
    return pl.ds(pl.multiple_of(block * size, size), size)


def kernel(
    rhs_hbm, root_hbm, inv_hbm, cpl_hbm, rinv_hbm, counts_hbm, map_hbm,
    child_out, root_out,
    rhs_v, root_v, inv_v, cpl_v, rinv_v,
    inv_hi, inv_lo, cpl_hi, cpl_lo, rin_hi, rin_lo,
    vec_hl, place, place_t, cplt_hi, cplt_lo, rint_hi, rint_lo, root_t, fwd,
    part1, core1, rs1, full1,
    part5, core5, rs5, full5,
    spread_s, xyr2, upd_t,
    part3, core3, rs3, full3,
    back_s, xyr4, back_t,
    acc_b, acc_c,
    ypart, yrs, yfull,
    counts, map_ref, load_sem, out_sem,
    sent1, sent3, sent5,
    c1r, z1r, g1r, s1r, c3r, z3r, g3r, s3r, c5r, z5r, g5r, s5r,
    p2r, q2r, p4r, q4r, y6r, w6r,
):
    f = lax.axis_index("front")
    r = lax.axis_index("row")
    c = lax.axis_index("col")
    z = c // 2
    k = c % 2
    sib = (f, r, z * 2 + (1 - k))

    way = 1 - 2 * k

    def chip(d):
        return (z + way * d + 2 * NZ) % NZ

    def zdev(d):
        return (f, r, chip(d) * 2 + k)

    def xydev(df, dr):
        return ((f + df) % 4, (r + dr) % 4, c)

    def rcopy(src, dst, ss, rs, dev):
        return pltpu.make_async_remote_copy(
            src_ref=src, dst_ref=dst, send_sem=ss, recv_sem=rs, device_id=dev, device_id_type=MESH
        )

    def await_blocks(sem, count):
        at = inv_v.at[pl.ds(0, count * 16)]
        pltpu.make_async_copy(at, at, sem).wait()

    def await_quarters(sem, count):
        at = inv_v.at[pl.ds(0, count * 8)]
        pltpu.make_async_copy(at, at, sem).wait()

    def await_slabs(sem, count):
        at = cpl_v.at[pl.ds(0, count * 8)]
        pltpu.make_async_copy(at, at, sem).wait()

    def zat(step):
        return chip(far_first(step))

    def block_of(step):
        return (1 - k) * 8 + step if step < 8 else k * 8 + zat(step - 8)

    def inv_load(part):
        at = rows(jnp.where(k == 0, (part + 4) % 8, part), 256)
        return pltpu.make_async_copy(inv_hbm.at[0, at], inv_v.at[at], load_sem.at[(0, 0, 1, 1, 2, 2, 2, 2)[part]])

    rhs_load = pltpu.make_async_copy(rhs_hbm.at[0], rhs_v, load_sem.at[3])
    cpl_load = pltpu.make_async_copy(cpl_hbm.at[0], cpl_v, load_sem.at[4])
    rinv_load = pltpu.make_async_copy(rinv_hbm, rinv_v, load_sem.at[5])
    root_load = pltpu.make_async_copy(root_hbm, root_v, load_sem.at[6])
    counts_load = pltpu.make_async_copy(counts_hbm, counts, load_sem.at[7])
    map_load = pltpu.make_async_copy(map_hbm, map_ref, load_sem.at[8])
    counts_load.start()
    for i in range(4):
        at = pl.ds(i * BLK, BLK)
        pltpu.make_async_copy(rhs_hbm.at[0, at], rhs_v.at[at], load_sem.at[3]).start()
    for part in range(8):
        inv_load(part).start()
    map_load.start()
    cpl_load.start()
    rinv_load.start()
    root_load.start()

    barrier = pltpu.get_barrier_semaphore()
    pl.semaphore_signal(barrier, inc=1, device_id=sib, device_id_type=MESH)
    for d in range(1, NZ):
        pl.semaphore_signal(barrier, inc=1, device_id=zdev(d), device_id_type=MESH)
    for e in range(1, NXY):
        pl.semaphore_signal(barrier, inc=1, device_id=xydev(e // 4, e % 4), device_id_type=MESH)


    counts_load.wait()
    count = counts[f]
    own = k * 8 + z
    rhs_load.wait()
    spot = c * 512 + lax.broadcasted_iota(jnp.int32, (512, BLK), 0)
    vector = jnp.concatenate(split(jnp.where(spot < count, rhs_v[...], 0.0)), axis=1)
    vec_hl[:512, :] = vector
    vec_hl[512:, :] = vector


    def z_reduce(part, rs, zs, zr):
        def copy(index, src, d):
            return rcopy(src, rs.at[index], zs, zr.at[(0, 0, 1, 2, 2, 2, 2)[index]], zdev(d))

        def send(step):
            index = {0: 0, 1: 1, 2: 2, 5: 3, 6: 4}[step]
            return copy(index, part(zat(step)), {0: 2, 1: 1, 2: -1, 5: 1, 6: -1}[step])

        def arrived(begin, end, sem):
            at = rs.at[pl.ds(begin, end - begin)]
            pltpu.make_async_copy(at, at, zr.at[sem]).wait()

        def relay():
            arrived(0, 2, 0)
            part(chip(2))[...] += rs[0] + rs[1]
            copy(5, part(chip(2)), 2).start()
            arrived(2, 3, 1)
            part(chip(-2))[...] += rs[2]
            copy(6, part(chip(-2)), -2).start()

        def total():
            arrived(3, 7, 2)
            return part(z)[...] + ((rs[3] + rs[4]) + (rs[5] + rs[6]))

        return send, relay, total

    def gather(piece, gs, gr, sr):
        def z_copy(index, d_owner, d):
            at = piece(k, chip(d_owner))
            return rcopy(at, at, gs, gr.at[(0, 1, 2, 2, 3, 3, 3)[index]], zdev(d))

        def sib_copy(owner, far):
            at = piece(k, owner)
            return rcopy(at, at, gs, sr.at[far], sib)

        first = [(0, 0, 2), (1, 0, -2), (2, 0, 1), (3, 0, -1)]
        second = [(4, -2, 1), (5, -2, 2), (6, 2, -1)]
        arrivals = {0: -2, 1: 2, 2: -1, 3: 1, 4: -3, 5: -4, 6: 3}

        def arrive(index):
            z_copy(index, arrivals[index], 1).wait_recv()

        def pass_on(index):
            sib_copy(chip(arrivals[index]), index // 4).start()

        def start():
            for item in first:
                z_copy(*item).start()
            sib_copy(z, 0).start()

        def relay():
            arrive(0)
            z_copy(*second[0]).start()
            z_copy(*second[1]).start()
            pass_on(0)
            arrive(1)
            z_copy(*second[2]).start()
            pass_on(1)

        def near():
            await_quarters(gr.at[2], 2)
            for index in (2, 3):
                pass_on(index)

        def far():
            await_quarters(gr.at[3], 3)
            for index in (6, 4, 5):
                pass_on(index)

        def take(far):
            await_quarters(sr.at[far], (5, 3)[far])
            return [chip(d) for d in (ARRIVALS[:5], ARRIVALS[5:])[far]]

        return start, relay, near, far, take

    def z_reduce_direct(part, rs, zs, zr):
        def start():
            for step in range(7):
                rcopy(part(zat(step)), rs.at[step], zs, zr, zdev(far_first(step))).start()

        def total():
            pltpu.make_async_copy(rs, rs, zr).wait()
            value = part(z)[...]
            for step in range(7):
                value = value + rs[step]
            return value

        return start, total

    def gather_direct(piece, gs, gr, sr):
        def z_copy(step, owner):
            at = piece(k, owner)
            return rcopy(at, at, gs, gr.at[step], zdev(far_first(step)))

        def sib_copy(owner):
            at = piece(k, owner)
            return rcopy(at, at, gs, sr, sib)

        def start():
            for step in range(7):
                z_copy(step, z).start()
            sib_copy(z).start()

        def finish():
            for step in (5, 6, 3, 4, 1, 2, 0):
                owner = chip(-far_first(step))
                z_copy(step, owner).wait_recv()
                sib_copy(owner).start()
            await_slabs(sr, NZ)

        return start, finish


    def slab(p):
        return p % 2, rows(p // 2, 8)

    def plane_at(df, dr):
        return slab(((f + df) % 4) * 4 + (r + dr) % 4)

    here = plane_at(0, 0)

    def plane(src, recv, full, ps, pr, qr):
        def out_copy(step):
            df, dr = PLANE[step]
            return rcopy(src.at[plane_at(df, dr)], recv.at[step], ps, pr, xydev(df, dr))

        def all_copy(step):
            df, dr = PLANE[step]
            return rcopy(full.at[here], full.at[here], ps, qr, xydev(df, dr))

        def start():
            for step in range(15):
                out_copy(step).start()

        def middle(combine):
            total = src[here]
            pltpu.make_async_copy(recv, recv, pr).wait()
            for step in range(15):
                total = total + recv[step]
            full[here] = combine(total)
            for step in range(15):
                all_copy(step).start()

        def finish():
            await_slabs(qr, 15)
            return join(full[0], full[1], 1)

        return start, middle, finish


    def forward_group(group):
        steps = range(4 * group, 4 * group + 4)
        if group < 3:
            at = inv_v.at[pl.ds(0, (512, 512, 1024)[group])]
            pltpu.make_async_copy(at, at, load_sem.at[group]).wait()
        highs, lows = [], []
        for step in steps:
            at = rows(block_of(step))
            high, low = split(inv_v[at, :])
            highs.append(high)
            lows.append(low)
        values = []
        for high, low in zip(highs, lows):
            value = mm(join(high, low, 1), vec_hl[...])
            values.append((value[:, :BLK] + value[:, BLK:]).T)
        return values

    core_copy1 = rcopy(part1.at[rows(1 - k, 8)], core1, sent1, c1r, sib)

    for group in range(2):
        for j, value in enumerate(forward_group(group)):
            part1[block_of(4 * group + j)] = value
    pl.semaphore_wait(barrier, NZ + NXY - 1)
    core_copy1.start()

    quarter = [pl.ds((q % 2) * QSRC, QSRC) for q in range(4)]
    sum1 = [
        z_reduce(lambda owner, q=q: part1.at[k * 8 + owner, pl.ds(q * QSRC, QSRC)], rs1.at[q], sent1, z1r.at[q])
        for q in range(4)
    ]
    for group in range(2):
        values = forward_group(group + 2)
        if not group:
            core_copy1.wait_recv()
        for j in range(4):
            owner = zat(4 * group + j)
            part1[k * 8 + owner] = values[j] + core1[owner]
        for step in ((0, 1, 2), (5, 6))[group]:
            for q in (0, 1):
                sum1[q][0](step).start()
    for step in (0, 1, 2, 5, 6):
        for q in (2, 3):
            sum1[q][0](step).start()

    cpl_load.wait()

    def split_cpl(i):
        at = rows(i)
        high, low = split(cpl_v[at, :])
        cpl_hi[at, :] = high
        cpl_lo[at, :] = low

    loop(16, split_cpl)

    def build_map(i):
        at = rows(i)
        spots = i * BLK + lax.broadcasted_iota(jnp.int32, (BLK, 384), 0)
        hot = (map_ref[...] - c * 768 == spots).astype(F32)
        place[at, :] = hot.astype(BF16)
        place_t[i] = hot.T.astype(BF16)

    map_load.wait()
    loop(6, build_map)

    def split_rinv(i):
        at = rows(i)
        value = rinv_v[at, :]
        high, low = split(value)
        rin_hi[at, :] = high
        rin_lo[at, :] = low
        high, low = split(value.T)
        rint_hi[i] = high
        rint_lo[i] = low

    def split_inv(i):
        at = rows(i)
        high, low = split(inv_v[at, :])
        inv_hi[at, :] = high
        inv_lo[at, :] = low

    def turn_cpl(i):
        high, low = split(cpl_v[rows(i), :].T)
        cplt_hi[i] = high
        cplt_lo[i] = low

    root_load.wait()
    for i in range(6):
        turned = root_v[i * BLK:(i + 1) * BLK, :].T
        for h in range(2):
            root_t[h, i // 3, :, (i % 3) * BLK:(i % 3 + 1) * BLK] = turned[h * SRC:(h + 1) * SRC]
    live = r * 2048 + own * BLK + lax.broadcasted_iota(jnp.int32, (QSRC, BLK), 1) < count

    ag1, xy2, ag3, xy4, ag5 = [], [], [], [], []
    for q in range(4):
        sum1[q][1]()
    rinv_load.wait()
    loop(6, split_rinv)
    for q in range(4):
        forward = jnp.where(live, sum1[q][2](), 0.0)
        fwd[q // 2, quarter[q], :] = forward
        full1[q // 2, own, quarter[q], :] = forward
        ag1.append(gather(
            lambda kk, zz, q=q: full1.at[q // 2, kk * 8 + zz, quarter[q]], sent1, g1r.at[q], s1r.at[q]
        ))
        ag1[q][0]()

    def use_border(h):
        def use(owners):
            blocks = [side * 8 + owner for owner in owners for side in (k, 1 - k)]
            left = stack(jnp.concatenate([full1[h, block] for block in blocks], axis=1))
            high = jnp.concatenate([cpl_hi[rows(block), :] for block in blocks], axis=0)
            low = jnp.concatenate([cpl_lo[rows(block), :] for block in blocks], axis=0)
            return mm_split(left, high, low)

        return use

    for q in range(4):
        ag1[q][1]()
    for q in range(4):
        ag1[q][2]()
    for h in range(2):
        for q in (2 * h, 2 * h + 1):
            ag1[q][3]()
        owners = [ag1[q][4](0) for q in (2 * h, 2 * h + 1)][0]
        acc_b[...] = use_border(h)(owners)
        owners = [ag1[q][4](1) for q in (2 * h, 2 * h + 1)][0]
        whole = halves(acc_b[...] + use_border(h)(owners))
        border_hl = stack(whole)
        spread = halves(mm(border_hl, jnp.concatenate([place_t[i] for i in range(6)], axis=1)))
        spread_s[h, 0] = spread[:, :384]
        spread_s[h, 1] = spread[:, 384:]
        xy2.append(plane(
            spread_s.at[h], xyr2.at[h], upd_t.at[h], sent3, p2r.at[h], q2r.at[h]
        ))
        xy2[h][0]()

    loop(8, turn_cpl)
    for h in range(2):
        xy2[h][1](lambda total, h=h: root_t.at[h][here] - total)

    def core_copy3(h):
        return rcopy(
            part3.at[h, 1 - k], core3.at[h], sent3, c3r.at[h], sib
        )

    def slab3(kk, zz):
        return kk, rows(zz, 8)

    loop(8, lambda i: turn_cpl(i + 8))
    sum3 = []
    for h in range(2):
        upd_hl = stack(xy2[h][2]())
        for side in (1 - k, k):
            blocks = [side * 3 + i for i in range(3)]
            part3[h, side] = halves(
                mm_split(
                    upd_hl,
                    jnp.concatenate([rint_hi[block] for block in blocks], axis=1),
                    jnp.concatenate([rint_lo[block] for block in blocks], axis=1),
                )
            )
            if side is not k:
                core_copy3(h).start()
        core_copy3(h).wait_recv()
        part3[h, k] += core3[h]
        sum3.append(z_reduce_direct(
            lambda owner, h=h: part3.at[h].at[slab3(k, owner)], rs3.at[h], sent3, z3r.at[h]
        ))
        sum3[h][0]()
    loop(16, split_inv)
    for h in range(2):
        full3.at[h][slab3(k, z)] = sum3[h][1]()
        ag3.append(gather_direct(
            lambda kk, zz, h=h: full3.at[h].at[slab3(kk, zz)], sent3, g3r.at[h], s3r.at[h]
        ))
        ag3[h][0]()

    for h in range(2):
        ag3[h][1]()
        fwd_hl = stack(join(full3[h, 0], full3[h, 1], 1))
        value = halves(mm_split(fwd_hl, rin_hi[...], rin_lo[...]))
        back_s[h, 0] = value[:, :384]
        back_s[h, 1] = value[:, 384:]
        xy4.append(plane(
            back_s.at[h], xyr4.at[h], back_t.at[h], sent3, p4r.at[h], q4r.at[h]
        ))
        xy4[h][0]()
    for h in range(2):
        xy4[h][1](lambda total: total)

    def core_copy5(h, group):
        src = part5.at[h, rows(2 * (1 - k) + group, 4)]
        return rcopy(src, core5.at[h, pl.ds(4 * group, 4)], sent5, c5r.at[h], sib)

    sum5 = []
    for h in range(2):
        back = xy4[h][2]()
        left = stack(halves(mm(stack(back), place[...])))

        def correction_group(group, left=left):
            blocks = [block_of(step) for step in range(4 * group, 4 * group + 4)]
            value = halves(
                mm_split(
                    left,
                    jnp.concatenate([cplt_hi[block] for block in blocks], axis=1),
                    jnp.concatenate([cplt_lo[block] for block in blocks], axis=1),
                )
            )
            return [value[:, j * BLK:(j + 1) * BLK] for j in range(4)]

        for group in range(2):
            for j, value in enumerate(correction_group(group)):
                part5[h, block_of(4 * group + j)] = value
            core_copy5(h, group).start()
        for q in (2 * h, 2 * h + 1):
            sum5.append(z_reduce(
                lambda owner, q=q: part5.at[q // 2, k * 8 + owner, quarter[q]], rs5.at[q], sent5, z5r.at[q]
            ))
        values = correction_group(2) + correction_group(3)
        for step in range(8):
            part5[h, block_of(step + 8)] = values[step]
        pltpu.make_async_copy(core5.at[h], core5.at[h], c5r.at[h]).wait()
        for step in range(8):
            owner = zat(step)
            part5[h, k * 8 + owner] += core5[h, owner]
            if step in (0, 1, 2, 5, 6):
                for q in (2 * h, 2 * h + 1):
                    sum5[q][0](step).start()

    for i in range(6):
        half, at = i // 3, (i % 3) * BLK
        root_v[i * BLK:(i + 1) * BLK, :] = join(back_t[0, half, :, at:at + BLK], back_t[1, half, :, at:at + BLK], 0).T
    root_store = pltpu.make_async_copy(root_v, root_out, out_sem.at[0])
    root_store.start()

    for q in range(4):
        sum5[q][1]()
    for q in range(4):
        rest = fwd[q // 2, quarter[q], :] - sum5[q][2]()
        full5[q // 2, own, quarter[q], :] = jnp.where(live, rest, 0.0)
        ag5.append(gather(
            lambda kk, zz, q=q: full5.at[q // 2, kk * 8 + zz, quarter[q]], sent5, g5r.at[q], s5r.at[q]
        ))
        ag5[q][0]()

    def yslab(d):
        return rows((r + d) % 4, 16)

    def ydev(d):
        return (f, (r + d) % 4, c)

    def y_copy(h, d):
        return rcopy(ypart.at[h, yslab(d)], yrs.at[h, d - 1], sent5, y6r.at[h], ydev(d))

    def w_copy(h, d):
        return rcopy(yfull.at[h, yslab(0)], yfull.at[h, yslab(0)], sent5, w6r.at[h], ydev(d))

    def use_back(h):
        def use(owners):
            blocks = [side * 8 + owner for owner in owners for side in (k, 1 - k)]
            left = stack(jnp.concatenate([full5[h, block] for block in blocks], axis=1))
            high = jnp.concatenate([inv_hi[rows(block), :] for block in blocks], axis=0)
            low = jnp.concatenate([inv_lo[rows(block), :] for block in blocks], axis=0)
            return mm_split(left, high, low)

        return use

    for q in range(4):
        ag5[q][1]()
    for q in range(4):
        ag5[q][2]()
    for h in range(2):
        for q in (2 * h, 2 * h + 1):
            ag5[q][3]()
        owners = [ag5[q][4](0) for q in (2 * h, 2 * h + 1)][0]
        acc_c[...] = use_back(h)(owners)
        owners = [ag5[q][4](1) for q in (2 * h, 2 * h + 1)][0]
        whole = halves(acc_c[...] + use_back(h)(owners))
        ypart[h] = whole
        for d in (2, 1, 3):
            y_copy(h, d).start()
    for h in range(2):
        total = ypart[h, yslab(0)]
        pltpu.make_async_copy(yrs.at[h], yrs.at[h], y6r.at[h]).wait()
        for d in (1, 3, 2):
            total = total + yrs[h, d - 1]
        yfull[h, yslab(0)] = total
        for d in (2, 1, 3):
            w_copy(h, d).start()
    for h in range(2):
        await_blocks(w6r.at[h], 3)
    for i in range(4):
        at = c * 512 + i * BLK + lax.broadcasted_iota(jnp.int32, (BLK, BLK), 0)
        value = join(yfull[0, :, i * BLK:(i + 1) * BLK], yfull[1, :, i * BLK:(i + 1) * BLK], 0).T
        rhs_v[i * BLK:(i + 1) * BLK, :] = jnp.where(at < count, value, 0.0)
        part = pl.ds(i * BLK, BLK)
        pltpu.make_async_copy(rhs_v.at[part], child_out.at[0, part], out_sem.at[1]).start()
    child_store = pltpu.make_async_copy(rhs_v, child_out.at[0], out_sem.at[1])
    await_blocks(sent1, 8 * 2 + 2 * 7 + 2 * 15)
    await_slabs(sent3, 2 * 30 + 2 * 8 + 2 * 7 + 2 * 15 + 2 * 30)
    await_blocks(sent5, 2 * 8 + 2 * 7 + 2 * 15 + 2 * 6)
    root_store.wait()
    child_store.wait()


def hand_over(child, root, child_out, root_out, child_v, root_v, sems):
    loads = [
        pltpu.make_async_copy(child, child_v, sems.at[0]),
        pltpu.make_async_copy(root, root_v, sems.at[1]),
    ]
    stores = [
        pltpu.make_async_copy(child_v, child_out, sems.at[2]),
        pltpu.make_async_copy(root_v, root_out, sems.at[3]),
    ]
    for load in loads:
        load.start()
    for load, store in zip(loads, stores):
        load.wait()
        store.start()
    for store in stores:
        store.wait()


def per_device(child_rhs, root_rhs, child_inv, coupling, root_inv, pivot_counts, border_map):
    def v(*shape, dtype=F32):
        return pltpu.VMEM(shape, dtype)

    dma = pltpu.SemaphoreType.DMA
    scratch = [
        v(512, 128), v(768, 128), v(2048, 512), v(2048, 384), v(768, 768),
        v(2048, 512, dtype=BF16), v(2048, 512, dtype=BF16), v(2048, 384, dtype=BF16), v(2048, 384, dtype=BF16),
        v(768, 768, dtype=BF16), v(768, 768, dtype=BF16),
        v(1024, 256, dtype=BF16), v(768, 384, dtype=BF16), v(6, 384, 128, dtype=BF16),
        v(16, 384, 128, dtype=BF16), v(16, 384, 128, dtype=BF16),
        v(6, 768, 128, dtype=BF16), v(6, 768, 128, dtype=BF16), v(2, 2, 64, 384), v(2, 64, 128),
        v(16, 128, 128), v(8, 128, 128), v(4, 7, 32, 128), v(2, 16, 64, 128),
        v(2, 16, 64, 128), v(2, 8, 64, 128), v(4, 7, 32, 128), v(2, 16, 64, 128),
        v(2, 2, 64, 384), v(2, 15, 8, 384), v(2, 2, 64, 384),
        v(2, 2, 64, 384), v(2, 64, 384), v(2, 7, 8, 384), v(2, 2, 64, 384),
        v(2, 2, 64, 384), v(2, 15, 8, 384), v(2, 2, 64, 384),
        v(128, 384), v(128, 512),
        v(2, 64, 512), v(2, 3, 16, 512), v(2, 64, 512),
        pltpu.SMEM((4,), jnp.int32), pltpu.VMEM((1, 384), jnp.int32), dma((9,)), dma((2,)),
    ]
    scratch += [dma] * 3
    scratch += [dma, dma((4, 3)), dma((4, 4)), dma((4, 2))]
    scratch += [dma((2,)), dma((2,)), dma((2, 7)), dma((2,))]
    scratch += [dma((2,)), dma((4, 3)), dma((4, 4)), dma((4, 2))]
    scratch += [dma((2,))] * 6
    hbm = pl.BlockSpec(memory_space=pl.ANY)
    results = tuple(
        pl.pallas_call(
            kernel,
            out_shape=(
                jax.ShapeDtypeStruct((1, 512, 128), F32),
                jax.ShapeDtypeStruct((768, 128), F32),
            ),
            in_specs=[hbm] * 7,
            out_specs=(hbm, hbm),
            scratch_shapes=scratch,
            compiler_params=pltpu.CompilerParams(
                collective_id=0, has_side_effects=True, vmem_limit_bytes=56 << 20
            ),
            cost_estimate=pl.CostEstimate(flops=5 * 10**9, bytes_accessed=11 * 10**6, transcendentals=0),
        )(child_rhs, root_rhs, child_inv, coupling, root_inv, pivot_counts, border_map)
    )
    return tuple(
        pl.pallas_call(
            hand_over,
            out_shape=tuple(jax.ShapeDtypeStruct(a.shape, a.dtype) for a in results),
            in_specs=[hbm] * 2,
            out_specs=(hbm, hbm),
            scratch_shapes=[v(1, 512, 128), v(768, 128), dma((4,))],
            compiler_params=pltpu.CompilerParams(vmem_limit_bytes=56 << 20),
        )(*results)
    )


def solution(mesh):
    in_specs = (
        P("front", "col", None),
        P("col", None),
        P("front", "row", "col"),
        P("front", "row", "col"),
        P(("front", "row"), "col"),
        P(),
        P("front", "col"),
    )
    out_specs = (P("front", "col", None), P("col", None))
    return jax.shard_map(
        per_device, mesh=mesh, in_specs=in_specs, out_specs=out_specs, check_vma=False
    )
```
